512 devices in a mesh: dp: 32 (over x, z), pipe: 16 (over y, core).
Axes of the slice: x: 4, y: 8, z: 8, core: 2. Of those that a mesh axis runs over, the one named last changes fastest.
Arguments:
- hidden: bfloat16 [2, 768, 5376], P(None, 'dp', 'pipe'), may hold values from -64 to 64
- norm_gain: float32 [5376], replicated, may hold values from 0.1 to 1.9
- embedding: bfloat16 [131072, 5376], P(('dp', 'pipe')), may hold values from -4 to 4
- targets: int32 [2, 768], P(None, 'dp'), may hold values from 0 to 131071
Outputs:
- token_loss: float32 [2, 768], P(None, 'dp')
The draws below stay inside these ranges and needn't reach their ends.
All inputs are finite; a program needn't handle non-finite values.
Results may differ from the reference program's by a relative error of at most 0.00054.
Values may be sent and summed in bfloat16 or wider, within the bound.
No kernel may reach another device: no remote copies, remote signals or barrier semaphores. Data moves between devices by JAX's collectives and lax.ppermute only.
A program may use at most 64 MiB of HBM per device.

```python
import math
import jax
import jax.numpy as jnp
from jax import lax

H = 5376
V_DEV = 256
MICRO = 2
TOK_MB = 768
VOCAB = 131072
N_DP = 32
N_PIPE = 16


def shared_rows(key):
    return jnp.clip(jax.random.normal(jax.random.fold_in(key, 5), (MICRO, TOK_MB, H), jnp.float32), -5.0, 5.0)


def draw_hidden(key, part):
    common = shared_rows(key)
    return common.astype(jnp.bfloat16)


def draw_embedding(key, part):
    key = jax.random.fold_in(key, 2)
    keys = jax.random.split(key, 2)
    row_scale = jnp.exp(jax.random.uniform(keys[0], (VOCAB, 1), jnp.float32, math.log(1.5), math.log(5.0)))
    entries = jnp.clip(jax.random.normal(keys[1], (VOCAB, H), jnp.float32), -5.0, 5.0)
    result = entries * row_scale / math.sqrt(H)
    return result.astype(jnp.bfloat16)


def place_ends(array, stream_key, least, largest):
    extent = array.shape
    spot = [jax.random.randint(jax.random.fold_in(stream_key, axis), (), 0, extent[axis]) for axis in range(len(extent))]
    array = array.at[tuple(spot)].set(least)
    longest = extent.index(max(extent))
    spot[longest] = (spot[longest] + 1) % extent[longest]
    return array.at[tuple(spot)].set(largest)


def setup_inputs(seed: int = 0) -> dict:
    key_list = jax.random.split(jax.random.key(seed), 5)
    hidden = draw_hidden(jax.random.fold_in(key_list[4], 71), 0)
    norm_gain = jnp.clip(1.0 + 0.18 * jax.random.normal(key_list[1], (H,), jnp.float32), 0.1, 1.9)
    embedding = draw_embedding(jax.random.fold_in(key_list[4], 71), 0)
    targets = place_ends(jax.random.randint(key_list[3], (MICRO, TOK_MB), 0, VOCAB), jax.random.fold_in(key_list[3], 1), 0, VOCAB - 1).astype(jnp.int32)
    return {"hidden": hidden, "norm_gain": norm_gain, "embedding": embedding, "targets": targets}


epsilon = 1e-06

def normalize(hidden, norm_gain):
    as_float = hidden.astype(jnp.float32)
    mean_square = lax.optimization_barrier(jnp.mean(as_float * as_float, axis=-1, keepdims=True))
    return (as_float * lax.rsqrt(mean_square + epsilon) * norm_gain).astype(jnp.bfloat16)

def reference(hidden, norm_gain, embedding, targets):
    normed = normalize(hidden, norm_gain).reshape(MICRO * TOK_MB, H)
    flat_targets = targets.reshape(MICRO * TOK_MB)
    block_rows = V_DEV * N_PIPE

    def visit(carried, block_index):
        running_max, running_sum, running_pick = carried
        weights = lax.dynamic_slice_in_dim(embedding, block_index * block_rows, block_rows, 0)
        logits = jnp.dot(normed, weights.T, preferred_element_type=jnp.float32)
        new_max = jnp.maximum(running_max, lax.optimization_barrier(jnp.max(logits, axis=1)))
        running_sum = running_sum * jnp.exp(running_max - new_max) + lax.optimization_barrier(jnp.sum(jnp.exp(logits - new_max[:, None]), axis=1))
        columns = block_index * block_rows + lax.broadcasted_iota(jnp.int32, (1, block_rows), 1)
        running_pick = running_pick + lax.optimization_barrier(jnp.sum(jnp.where(flat_targets[:, None] == columns, logits, 0.0), axis=1))
        return ((new_max, running_sum, running_pick), None)
    count = MICRO * TOK_MB
    start_state = (jnp.full((count,), -jnp.inf, jnp.float32), jnp.zeros((count,), jnp.float32), jnp.zeros((count,), jnp.float32))
    final_state, unused = lax.scan(visit, start_state, jnp.arange(N_DP, dtype=jnp.int32))
    row_max, row_sum, row_pick = final_state
    token_loss = row_max + jnp.log(row_sum) - row_pick
    return token_loss.reshape(MICRO, TOK_MB)
```

```python
import jax
import jax.numpy as jnp
import numpy as np
from jax import lax
from jax.experimental import pallas as pl
from jax.experimental.pallas import tpu as pltpu
from jax.sharding import Mesh
from jax.sharding import PartitionSpec as P

epsilon = 1e-06
H = 5376
PART = 672
FULL = 640
REM = PART - FULL
NY = 8
SOURCES = 16
TOKENS = SOURCES * 24
PAIRS = SOURCES // 2
PAIR_ROWS = 256
VOCAB_LOCAL = 256
EARLY = 48
WORDS = 4 * VOCAB_LOCAL
SMALL = pltpu.CompilerParams(vmem_limit_bytes=8 * 1024 * 1024)


def loss_kernel(*refs):
    g_any, blocks = refs[0], refs[1:5]
    gain_ref, target_ref, place_ref, out_ref, g, e, xn, logits, g_sem, e_sem = refs[5:]

    def g_copy(pair):
        rows = pl.ds(pl.multiple_of(pair * PAIR_ROWS, PAIR_ROWS), PAIR_ROWS)
        return pltpu.make_async_copy(g_any.at[:, rows, :], g.at[:, rows, :], g_sem.at[pair])

    for pair in range(PAIRS):
        g_copy(pair).start()
    e_copies, first_row = [], 0
    for i, block in enumerate(blocks):
        words = slice(first_row, first_row + block.shape[0])
        e_copies.append(pltpu.make_async_copy(block, e.at[words, :], e_sem.at[i]))
        first_row += block.shape[0]
    for copy in e_copies:
        copy.start()
    lane = lax.broadcasted_iota(jnp.int32, (16, 128), 1)

    def pair_step(pair, carry):
        g_copy(pair).wait()
        base = pair * PAIR_ROWS

        def tile(y, row):
            rows = pl.ds(pl.multiple_of(base + row, 16), 16)
            return g[y, rows, :].astype(jnp.float32)

        rest = [tile(y, 240) for y in range(NY)]
        for group in range(3):
            last = []
            for half in range(2):
                joined = None
                for q in range(4):
                    moved = rest[half * 4 + q]
                    shift = (q - group) * 32 % 128
                    if shift:
                        moved = pltpu.roll(moved, shift, 1)
                    joined = moved if joined is None else jnp.where(lane >= q * 32, moved, joined)
                last.append(joined)
            square = last[0] * last[0] + last[1] * last[1]
            for y in range(NY):
                for j in range(5):
                    value = tile(y, j * 48 + group * 16)
                    square = square + value * value
            scale = lax.rsqrt(jnp.sum(square, axis=1, keepdims=True) / H + epsilon)
            rows = pl.ds(pl.multiple_of(pair * 48 + group * 16, 16), 16)
            for y in range(NY):
                for j in range(5):
                    k = (y * 5 + j) * 128
                    value = tile(y, j * 48 + group * 16)
                    xn[rows, k : k + 128] = (value * scale * gain_ref[0:1, k : k + 128]).astype(jnp.bfloat16)
            for half in range(2):
                k = NY * FULL + half * 128
                xn[rows, k : k + 128] = (last[half] * scale * gain_ref[0:1, k : k + 128]).astype(jnp.bfloat16)
        return carry

    lax.fori_loop(0, PAIRS, pair_step, 0)

    for words, arrivals in ((slice(0, WORDS // 2), e_copies[:2]), (slice(WORDS // 2, WORDS), e_copies[2:])):
        for copy in arrivals:
            copy.wait()
        logits[:, words] = lax.dot_general(
            xn[...], e[words, :], (((1,), (1,)), ((), ())), preferred_element_type=jnp.float32
        )

    lane = lax.broadcasted_iota(jnp.int32, (48, 128), 1)
    stats = []
    for step in range(TOKENS // 48):
        rows = pl.ds(step * 48, 48)
        parts = [logits[rows, i * 128 : (i + 1) * 128] for i in range(WORDS // 128)]
        peak = parts[0]
        for part in parts[1:]:
            peak = jnp.maximum(peak, part)
        peak = jnp.max(peak, axis=1, keepdims=True)
        target = target_ref[rows, :]
        total = jnp.zeros((48, 128), jnp.float32)
        picked = jnp.zeros((48, 128), jnp.float32)
        for i, part in enumerate(parts):
            total = total + jnp.exp(part - peak)
            picked = picked + jnp.where(target - (place_ref[i // 2] + i % 2 * 128) == lane, part, 0.0)
        total = jnp.sum(total, axis=1, keepdims=True)
        picked = jnp.sum(picked, axis=1, keepdims=True)
        stats.append(jnp.where(lane == 0, peak, jnp.where(lane == 1, total, picked)))
    stats = jnp.concatenate(stats, axis=0)
    for i in range(TOKENS // 128):
        out_ref[:, i * 128 : (i + 1) * 128] = stats[i * 128 : (i + 1) * 128, :].T[0:8, :]


def local_losses(gathered, blocks, gain, target, place):
    any_space = pl.BlockSpec(memory_space=pl.ANY)
    vmem = pl.BlockSpec(memory_space=pltpu.VMEM)
    gathered = pltpu.with_memory_space_constraint(gathered, pltpu.HBM)
    blocks = [pltpu.with_memory_space_constraint(a, pltpu.HBM) for a in blocks]
    return pl.pallas_call(
        loss_kernel,
        out_shape=jax.ShapeDtypeStruct((8, TOKENS), jnp.float32),
        in_specs=[any_space] * 5 + [vmem, vmem, pl.BlockSpec(memory_space=pltpu.SMEM)],
        out_specs=vmem,
        scratch_shapes=[
            pltpu.VMEM((NY, PAIRS * PAIR_ROWS, 128), jnp.bfloat16),
            pltpu.VMEM((WORDS, H), jnp.bfloat16),
            pltpu.VMEM((TOKENS, H), jnp.bfloat16),
            pltpu.VMEM((TOKENS, WORDS), jnp.float32),
            pltpu.SemaphoreType.DMA((PAIRS,)),
            pltpu.SemaphoreType.DMA((len(blocks),)),
        ],
        compiler_params=pltpu.CompilerParams(vmem_limit_bytes=32 * 1024 * 1024),
        cost_estimate=pl.CostEstimate(flops=2 * TOKENS * WORDS * H, bytes_accessed=16 * 1024 * 1024, transcendentals=TOKENS * WORDS),
    )(gathered, *blocks, gain, target, place)


def prepare_kernel(hidden_ref, targets_ref, out_ref):
    row = lax.broadcasted_iota(jnp.int32, (24, 24), 0)
    column = lax.broadcasted_iota(jnp.int32, (24, 24), 1)
    lane = lax.broadcasted_iota(jnp.int32, (24, 128), 1)
    for m in range(2):
        target = jnp.sum(jnp.where(row == column, targets_ref[m : m + 1, :], 0), axis=1, keepdims=True)
        digits = jnp.where(lane == 80, target & 127, jnp.where(lane == 81, (target >> 7) & 127, target >> 14))
        tail = jnp.pad(hidden_ref[m, :, 256:336].astype(jnp.float32), ((0, 0), (0, 48)))
        tail = jnp.where(lane < 80, tail, jnp.where(lane < 83, digits.astype(jnp.float32), 0.0))
        tail = tail.astype(jnp.bfloat16)
        for s in range(SOURCES):
            out_ref[2 * s + m, :, 0:256] = hidden_ref[m, :, 0:256]
            out_ref[2 * s + m, :, 256:384] = tail


def prepare(hidden, targets):
    hidden, targets = (pltpu.with_memory_space_constraint(a, pltpu.HBM) for a in (hidden, targets))
    return pl.pallas_call(
        prepare_kernel,
        out_shape=pltpu.HBM((2 * SOURCES, 24, 384), jnp.bfloat16),
        compiler_params=SMALL,
    )(hidden, targets)


def repack_kernel(got_ref, units_ref, target_ref):
    lane = lax.broadcasted_iota(jnp.int32, (48, 128), 1)
    short = lane[0:16]
    weight = jnp.where(lane == 80, 1, jnp.where(lane == 81, 128, jnp.where(lane == 82, 16384, 0))).astype(jnp.float32)

    def pair_step(pair, carry):
        def tile(c, j):
            both = [got_ref[4 * pair + 2 * d + c, :, j * 128 : (j + 1) * 128].astype(jnp.float32) for d in range(2)]
            return jnp.concatenate(both, axis=0)

        a, b = tile(0, 2), tile(1, 2)
        tiles = [tile(0, 0), tile(0, 1), tile(1, 0), tile(1, 1), jnp.where(lane < 80, a, pltpu.roll(b, 80, 1))]
        base = pair * PAIR_ROWS
        for j in range(5):
            rows = pl.ds(pl.multiple_of(base + j * 48, 16), 48)
            units_ref[rows, :] = tiles[j].astype(jnp.bfloat16)
        rest = [pltpu.roll(b[g * 16 : (g + 1) * 16], (32 * g - 48) % 128, 1) for g in range(3)]
        rest = jnp.where(short < 32, rest[0], jnp.where(short < 64, rest[1], jnp.where(short < 96, rest[2], 0.0)))
        units_ref[pl.ds(pl.multiple_of(base + 240, 16), 16), :] = rest.astype(jnp.bfloat16)
        target = jnp.sum(a * weight, axis=1, keepdims=True)
        target_ref[pl.ds(pl.multiple_of(pair * 48, 16), 48), :] = target.astype(jnp.int32)
        return carry

    lax.fori_loop(0, PAIRS, pair_step, 0)


def repack(got):
    return pl.pallas_call(
        repack_kernel,
        out_shape=(
            pltpu.HBM((PAIRS * PAIR_ROWS, 128), jnp.bfloat16),
            jax.ShapeDtypeStruct((TOKENS, 1), jnp.int32),
        ),
        compiler_params=SMALL,
        cost_estimate=pl.CostEstimate(flops=2000000, bytes_accessed=1200000, transcendentals=0),
    )(got)


def pieces():
    for y in range(NY):
        for begin, end in ((0, 256), (336, 592), (256, 336), (592, 640)):
            yield y * PART + begin, y * PART + end
    for y in range(NY):
        yield y * PART + FULL, (y + 1) * PART


def arrange(tiles, lane):
    def window(begin):
        k, shift = divmod(begin, 128)
        if shift == 0:
            return tiles[k]
        after = pltpu.roll(tiles[(k + 1) % len(tiles)], 128 - shift, 1)
        return jnp.where(lane < 128 - shift, pltpu.roll(tiles[k], 128 - shift, 1), after)

    out = []
    for y in range(NY):
        at = y * PART
        out += [window(at), window(at + 128), window(at + 336), window(at + 464)]
        out.append(jnp.where(lane < 80, window(at + 256), window(at + 592 - 80)))
    for half in range(2):
        joined = None
        for q in range(4):
            k, shift = divmod((half * 4 + q) * PART + FULL, 128)
            moved = tiles[k]
            if (q * 32 - shift) % 128:
                moved = pltpu.roll(moved, (q * 32 - shift) % 128, 1)
            joined = moved if joined is None else jnp.where(lane >= q * 32, moved, joined)
        out.append(joined)
    return out


def arrange_gain_kernel(gain_ref, out_ref):
    lane = lax.broadcasted_iota(jnp.int32, (8, 128), 1)
    tiles = [jnp.broadcast_to(gain_ref[:, k * 128 : (k + 1) * 128], (8, 128)) for k in range(H // 128)]
    for k, tile in enumerate(arrange(tiles, lane)):
        out_ref[:, k * 128 : (k + 1) * 128] = tile


def arrange_gain(gain):
    return pl.pallas_call(
        arrange_gain_kernel, out_shape=jax.ShapeDtypeStruct((8, H), jnp.float32), compiler_params=SMALL
    )(gain.reshape(1, H))


def reorder_kernel(*refs):
    out_ref = refs[-1]
    before = 0
    for ref in refs[:-1]:
        block = ref.shape[0]
        lane = lax.broadcasted_iota(jnp.int32, (16, 128), 1)

        def step(i, carry):
            src = pl.ds(pl.multiple_of(i * 16, 16), 16)
            dst = pl.ds(pl.multiple_of(before + i * 16, 16), 16)
            tiles = [ref[src, k * 128 : (k + 1) * 128].astype(jnp.float32) for k in range(H // 128)]
            for k, tile in enumerate(arrange(tiles, lane)):
                out_ref[dst, k * 128 : (k + 1) * 128] = tile.astype(jnp.bfloat16)
            return carry

        lax.fori_loop(0, block // 16, step, 0)
        before += block


def reorder_rows(*rows):
    count = sum(r.shape[0] for r in rows)
    return pl.pallas_call(
        reorder_kernel,
        out_shape=jax.ShapeDtypeStruct((count, H), jnp.bfloat16),
        compiler_params=pltpu.CompilerParams(vmem_limit_bytes=16 * 1024 * 1024),
        cost_estimate=pl.CostEstimate(flops=count * H * 8, bytes_accessed=count * H * 4, transcendentals=0),
    )(*rows)


def combine(peak, total, picked, axis):
    top = jnp.max(peak, axis=axis)
    total = jnp.sum(total * jnp.exp(peak - jnp.expand_dims(top, axis)), axis=axis)
    return top, total, jnp.sum(picked, axis=axis)


def per_device(hidden, norm_gain, embedding, targets):
    swap = [(0, 1), (1, 0)]
    tie = lax.optimization_barrier
    xh, xl, z, y, core = (lax.axis_index(a) for a in ("xh", "xl", "z", "y", "core"))

    def first_row(low, c):
        return ((((xh * 2 + low) * 8 + z) * 8 + y) * 2 + c) * VOCAB_LOCAL

    near, beside, far, far_beside = (first_row(low, c) for low in (xl, 1 - xl) for c in (core, 1 - core))
    place = jnp.stack([near, beside, far, far_beside])

    payload, embedding = tie((prepare(hidden, targets), embedding))
    got = lax.all_to_all(payload, ("xh", "z", "core"), 0, 0, tiled=True)
    units, target = repack(got)

    rows1 = lax.ppermute(embedding[:EARLY], "xl", swap)
    units, late, rows1, gain = tie((units, embedding, rows1, norm_gain))
    gathered = lax.all_gather(units, "y", axis=0)

    rows2 = lax.ppermute(late[EARLY:], "xl", swap)
    own = reorder_rows(late)
    beside_rows = lax.ppermute(own, "core", swap)
    far_rows = reorder_rows(rows1, rows2)
    far_beside_rows = lax.ppermute(far_rows, "core", swap)
    blocks = (own, beside_rows, far_rows, far_beside_rows)
    stats = local_losses(gathered, blocks, arrange_gain(gain), target, place)
    stats = stats[:3].reshape(3, SOURCES, 24).transpose(1, 0, 2)
    stats = lax.all_to_all(stats, ("xh", "z"), 0, 0, tiled=True)
    part = jnp.stack(combine(stats[:, 0], stats[:, 1], stats[:, 2], 0))
    every = lax.all_to_all(jnp.broadcast_to(part[None], (16, 3, 24)), ("y", "core"), 0, 0, tiled=True)
    every = every.reshape(NY, 2, 3, 24)
    peak, total, picked = combine(every[:, :, 0], every[:, :, 1], every[:, :, 2], 0)
    return peak + jnp.log(total) - picked


def solution(mesh):
    fine = Mesh(mesh.devices.reshape(2, 2, 8, 8, 2), ("xh", "xl", "z", "y", "core"))
    dp, pipe = ("xh", "xl", "z"), ("y", "core")
    placed = (P(None, dp, pipe), P(), P(dp + pipe, None), P(None, dp))
    return jax.shard_map(per_device, mesh=fine, in_specs=placed, out_specs=P(None, dp), check_vma=False)
```

```python
import jax
import jax.numpy as jnp
import numpy as np
from jax import lax
from jax.experimental import pallas as pl
from jax.experimental.pallas import tpu as pltpu
from jax.sharding import Mesh
from jax.sharding import PartitionSpec as P

epsilon = 1e-06
H = 5376
PART = 672
FULL = 640
REM = PART - FULL
NY = 8
SOURCES = 16
TOKENS = SOURCES * 24
PAIRS = SOURCES // 2
PAIR_ROWS = 256
VOCAB_LOCAL = 256
PIECE = VOCAB_LOCAL // 2
WORDS = 4 * VOCAB_LOCAL
SMALL = pltpu.CompilerParams(vmem_limit_bytes=8 * 1024 * 1024)


def loss_kernel(*refs):
    g_any, blocks = refs[0], refs[1:9]
    gain_ref, target_ref, place_ref, out_ref, g, e, xn, logits, g_sem, e_sem = refs[9:]

    def g_copy(pair):
        rows = pl.ds(pl.multiple_of(pair * PAIR_ROWS, PAIR_ROWS), PAIR_ROWS)
        return pltpu.make_async_copy(g_any.at[:, rows, :], g.at[:, rows, :], g_sem.at[pair])

    for pair in range(PAIRS):
        g_copy(pair).start()
    e_copies, first_row = [], 0
    for i, block in enumerate(blocks):
        words = slice(first_row, first_row + block.shape[0])
        e_copies.append(pltpu.make_async_copy(block, e.at[words, :], e_sem.at[i]))
        first_row += block.shape[0]
    for copy in e_copies:
        copy.start()
    lane = lax.broadcasted_iota(jnp.int32, (16, 128), 1)

    def pair_step(pair, carry):
        g_copy(pair).wait()
        base = pair * PAIR_ROWS

        def tile(y, row):
            rows = pl.ds(pl.multiple_of(base + row, 16), 16)
            return g[y, rows, :].astype(jnp.float32)

        rest = [tile(y, 240) for y in range(NY)]
        for group in range(3):
            last = []
            for half in range(2):
                joined = None
                for q in range(4):
                    moved = rest[half * 4 + q]
                    shift = (q - group) * 32 % 128
                    if shift:
                        moved = pltpu.roll(moved, shift, 1)
                    joined = moved if joined is None else jnp.where(lane >= q * 32, moved, joined)
                last.append(joined)
            square = last[0] * last[0] + last[1] * last[1]
            for y in range(NY):
                for j in range(5):
                    value = tile(y, j * 48 + group * 16)
                    square = square + value * value
            scale = lax.rsqrt(jnp.sum(square, axis=1, keepdims=True) / H + epsilon)
            rows = pl.ds(pl.multiple_of(pair * 48 + group * 16, 16), 16)
            for y in range(NY):
                for j in range(5):
                    k = (y * 5 + j) * 128
                    value = tile(y, j * 48 + group * 16)
                    xn[rows, k : k + 128] = (value * scale * gain_ref[0:1, k : k + 128]).astype(jnp.bfloat16)
            for half in range(2):
                k = NY * FULL + half * 128
                xn[rows, k : k + 128] = (last[half] * scale * gain_ref[0:1, k : k + 128]).astype(jnp.bfloat16)
        return carry

    lax.fori_loop(0, PAIRS, pair_step, 0)

    for words, arrivals in ((slice(0, WORDS // 2), e_copies[:4]), (slice(WORDS // 2, WORDS), e_copies[4:])):
        for copy in arrivals:
            copy.wait()
        logits[:, words] = lax.dot_general(
            xn[...], e[words, :], (((1,), (1,)), ((), ())), preferred_element_type=jnp.float32
        )

    lane = lax.broadcasted_iota(jnp.int32, (48, 128), 1)
    stats = []
    for step in range(TOKENS // 48):
        rows = pl.ds(step * 48, 48)
        parts = [logits[rows, i * 128 : (i + 1) * 128] for i in range(WORDS // 128)]
        peak = parts[0]
        for part in parts[1:]:
            peak = jnp.maximum(peak, part)
        peak = jnp.max(peak, axis=1, keepdims=True)
        target = target_ref[rows, :]
        total = jnp.zeros((48, 128), jnp.float32)
        picked = jnp.zeros((48, 128), jnp.float32)
        for i, part in enumerate(parts):
            total = total + jnp.exp(part - peak)
            picked = picked + jnp.where(target - place_ref[i] == lane, part, 0.0)
        total = jnp.sum(total, axis=1, keepdims=True)
        picked = jnp.sum(picked, axis=1, keepdims=True)
        stats.append(jnp.where(lane == 0, peak, jnp.where(lane == 1, total, picked)))
    stats = jnp.concatenate(stats, axis=0)
    for i in range(TOKENS // 128):
        out_ref[:, i * 128 : (i + 1) * 128] = stats[i * 128 : (i + 1) * 128, :].T[0:8, :]


def local_losses(gathered, blocks, gain, target, place):
    any_space = pl.BlockSpec(memory_space=pl.ANY)
    vmem = pl.BlockSpec(memory_space=pltpu.VMEM)
    gathered = pltpu.with_memory_space_constraint(gathered, pltpu.HBM)
    blocks = [pltpu.with_memory_space_constraint(a, pltpu.HBM) for a in blocks]
    return pl.pallas_call(
        loss_kernel,
        out_shape=jax.ShapeDtypeStruct((8, TOKENS), jnp.float32),
        in_specs=[any_space] * 9 + [vmem, vmem, pl.BlockSpec(memory_space=pltpu.SMEM)],
        out_specs=vmem,
        scratch_shapes=[
            pltpu.VMEM((NY, PAIRS * PAIR_ROWS, 128), jnp.bfloat16),
            pltpu.VMEM((WORDS, H), jnp.bfloat16),
            pltpu.VMEM((TOKENS, H), jnp.bfloat16),
            pltpu.VMEM((TOKENS, WORDS), jnp.float32),
            pltpu.SemaphoreType.DMA((PAIRS,)),
            pltpu.SemaphoreType.DMA((len(blocks),)),
        ],
        compiler_params=pltpu.CompilerParams(vmem_limit_bytes=32 * 1024 * 1024),
        cost_estimate=pl.CostEstimate(flops=2 * TOKENS * WORDS * H, bytes_accessed=16 * 1024 * 1024, transcendentals=TOKENS * WORDS),
    )(gathered, *blocks, gain, target, place)


def prepare_kernel(hidden_ref, targets_ref, out_ref):
    row = lax.broadcasted_iota(jnp.int32, (24, 24), 0)
    column = lax.broadcasted_iota(jnp.int32, (24, 24), 1)
    lane = lax.broadcasted_iota(jnp.int32, (24, 128), 1)
    for m in range(2):
        target = jnp.sum(jnp.where(row == column, targets_ref[m : m + 1, :], 0), axis=1, keepdims=True)
        digits = jnp.where(lane == 80, target & 127, jnp.where(lane == 81, (target >> 7) & 127, target >> 14))
        tail = jnp.pad(hidden_ref[m, :, 256:336].astype(jnp.float32), ((0, 0), (0, 48)))
        tail = jnp.where(lane < 80, tail, jnp.where(lane < 83, digits.astype(jnp.float32), 0.0))
        tail = tail.astype(jnp.bfloat16)
        for s in range(SOURCES):
            out_ref[2 * s + m, :, 0:256] = hidden_ref[m, :, 0:256]
            out_ref[2 * s + m, :, 256:384] = tail


def prepare(hidden, targets):
    hidden, targets = (pltpu.with_memory_space_constraint(a, pltpu.HBM) for a in (hidden, targets))
    return pl.pallas_call(
        prepare_kernel,
        out_shape=pltpu.HBM((2 * SOURCES, 24, 384), jnp.bfloat16),
        compiler_params=SMALL,
    )(hidden, targets)


def repack_kernel(got_ref, units_ref, target_ref):
    lane = lax.broadcasted_iota(jnp.int32, (48, 128), 1)
    short = lane[0:16]
    weight = jnp.where(lane == 80, 1, jnp.where(lane == 81, 128, jnp.where(lane == 82, 16384, 0))).astype(jnp.float32)

    def pair_step(pair, carry):
        def tile(c, j):
            both = [got_ref[4 * pair + 2 * d + c, :, j * 128 : (j + 1) * 128].astype(jnp.float32) for d in range(2)]
            return jnp.concatenate(both, axis=0)

        a, b = tile(0, 2), tile(1, 2)
        tiles = [tile(0, 0), tile(0, 1), tile(1, 0), tile(1, 1), jnp.where(lane < 80, a, pltpu.roll(b, 80, 1))]
        base = pair * PAIR_ROWS
        for j in range(5):
            rows = pl.ds(pl.multiple_of(base + j * 48, 16), 48)
            units_ref[rows, :] = tiles[j].astype(jnp.bfloat16)
        rest = [pltpu.roll(b[g * 16 : (g + 1) * 16], (32 * g - 48) % 128, 1) for g in range(3)]
        rest = jnp.where(short < 32, rest[0], jnp.where(short < 64, rest[1], jnp.where(short < 96, rest[2], 0.0)))
        units_ref[pl.ds(pl.multiple_of(base + 240, 16), 16), :] = rest.astype(jnp.bfloat16)
        target = jnp.sum(a * weight, axis=1, keepdims=True)
        target_ref[pl.ds(pl.multiple_of(pair * 48, 16), 48), :] = target.astype(jnp.int32)
        return carry

    lax.fori_loop(0, PAIRS, pair_step, 0)


def repack(got):
    return pl.pallas_call(
        repack_kernel,
        out_shape=(
            pltpu.HBM((PAIRS * PAIR_ROWS, 128), jnp.bfloat16),
            jax.ShapeDtypeStruct((TOKENS, 1), jnp.int32),
        ),
        compiler_params=SMALL,
        cost_estimate=pl.CostEstimate(flops=2000000, bytes_accessed=1200000, transcendentals=0),
    )(got)


def pieces():
    for y in range(NY):
        for begin, end in ((0, 256), (336, 592), (256, 336), (592, 640)):
            yield y * PART + begin, y * PART + end
    for y in range(NY):
        yield y * PART + FULL, (y + 1) * PART


def arrange(tiles, lane):
    def window(begin):
        k, shift = divmod(begin, 128)
        if shift == 0:
            return tiles[k]
        after = pltpu.roll(tiles[(k + 1) % len(tiles)], 128 - shift, 1)
        return jnp.where(lane < 128 - shift, pltpu.roll(tiles[k], 128 - shift, 1), after)

    out = []
    for y in range(NY):
        at = y * PART
        out += [window(at), window(at + 128), window(at + 336), window(at + 464)]
        out.append(jnp.where(lane < 80, window(at + 256), window(at + 592 - 80)))
    for half in range(2):
        joined = None
        for q in range(4):
            k, shift = divmod((half * 4 + q) * PART + FULL, 128)
            moved = tiles[k]
            if (q * 32 - shift) % 128:
                moved = pltpu.roll(moved, (q * 32 - shift) % 128, 1)
            joined = moved if joined is None else jnp.where(lane >= q * 32, moved, joined)
        out.append(joined)
    return out


def arrange_gain_kernel(gain_ref, out_ref):
    lane = lax.broadcasted_iota(jnp.int32, (8, 128), 1)
    tiles = [jnp.broadcast_to(gain_ref[:, k * 128 : (k + 1) * 128], (8, 128)) for k in range(H // 128)]
    for k, tile in enumerate(arrange(tiles, lane)):
        out_ref[:, k * 128 : (k + 1) * 128] = tile


def arrange_gain(gain):
    return pl.pallas_call(
        arrange_gain_kernel, out_shape=jax.ShapeDtypeStruct((8, H), jnp.float32), compiler_params=SMALL
    )(gain.reshape(1, H))


def reorder_kernel(ref, *out_refs):
    lane = lax.broadcasted_iota(jnp.int32, (16, 128), 1)
    for n, out_ref in enumerate(out_refs):

        def step(i, carry):
            src = pl.ds(pl.multiple_of(n * PIECE + i * 16, 16), 16)
            dst = pl.ds(pl.multiple_of(i * 16, 16), 16)
            tiles = [ref[src, k * 128 : (k + 1) * 128].astype(jnp.float32) for k in range(H // 128)]
            for k, tile in enumerate(arrange(tiles, lane)):
                out_ref[dst, k * 128 : (k + 1) * 128] = tile.astype(jnp.bfloat16)
            return carry

        lax.fori_loop(0, PIECE // 16, step, 0)


def reorder_rows(rows):
    piece = jax.ShapeDtypeStruct((PIECE, H), jnp.bfloat16)
    return pl.pallas_call(
        reorder_kernel,
        out_shape=(piece, piece),
        compiler_params=pltpu.CompilerParams(vmem_limit_bytes=16 * 1024 * 1024),
        cost_estimate=pl.CostEstimate(flops=VOCAB_LOCAL * H * 8, bytes_accessed=VOCAB_LOCAL * H * 4, transcendentals=0),
    )(rows)


def combine(peak, total, picked, axis):
    top = jnp.max(peak, axis=axis)
    total = jnp.sum(total * jnp.exp(peak - jnp.expand_dims(top, axis)), axis=axis)
    return top, total, jnp.sum(picked, axis=axis)


def per_device(hidden, norm_gain, embedding, targets):
    swap = [(0, 1), (1, 0)]
    tie = lax.optimization_barrier
    xh, xl, z, y, core = (lax.axis_index(a) for a in ("xh", "xl", "z", "y", "core"))

    x = xh * 2 + xl

    def first_row(at, c):
        return (((at % 4 * 8 + z) * 8 + y) * 2 + c) * VOCAB_LOCAL

    near = [first_row(x, c) + n * PIECE for c in (core, 1 - core) for n in range(2)]
    far = [first_row(x + 3 - 2 * n, c) + n * PIECE for c in (core, 1 - core) for n in range(2)]
    place = jnp.stack(near + far)

    payload, embedding = tie((prepare(hidden, targets), embedding))
    got = lax.all_to_all(payload, ("xh", "z", "core"), 0, 0, tiled=True)
    units, target = repack(got)

    units, late, gain = tie((units, embedding, norm_gain))
    gathered = lax.all_gather(units, "y", axis=0)

    low, high = reorder_rows(late)
    from_left = lax.ppermute(low, ("xh", "xl"), [(i, (i + 1) % 4) for i in range(4)])
    from_right = lax.ppermute(high, ("xh", "xl"), [(i, (i - 1) % 4) for i in range(4)])
    near, far = [low, high], [from_left, from_right]
    near += [lax.ppermute(rows, "core", swap) for rows in near]
    far += [lax.ppermute(rows, "core", swap) for rows in far]
    stats = local_losses(gathered, near + far, arrange_gain(gain), target, place)
    stats = stats[:3].reshape(3, SOURCES, 24).transpose(1, 0, 2)
    stats = lax.all_to_all(stats, ("xh", "z"), 0, 0, tiled=True)
    part = jnp.stack(combine(stats[:, 0], stats[:, 1], stats[:, 2], 0))
    every = lax.all_to_all(jnp.broadcast_to(part[None], (16, 3, 24)), ("y", "core"), 0, 0, tiled=True)
    every = every.reshape(NY, 2, 3, 24)
    peak, total, picked = combine(every[:, :, 0], every[:, :, 1], every[:, :, 2], 0)
    return peak + jnp.log(total) - picked


def solution(mesh):
    fine = Mesh(mesh.devices.reshape(2, 2, 8, 8, 2), ("xh", "xl", "z", "y", "core"))
    dp, pipe = ("xh", "xl", "z"), ("y", "core")
    placed = (P(None, dp, pipe), P(), P(dp + pipe, None), P(None, dp))
    return jax.shard_map(per_device, mesh=fine, in_specs=placed, out_specs=P(None, dp), check_vma=False)
```

```python
import jax
import jax.numpy as jnp
import numpy as np
from jax import lax
from jax.experimental import pallas as pl
from jax.experimental.pallas import tpu as pltpu
from jax.sharding import Mesh
from jax.sharding import PartitionSpec as P

epsilon = 1e-06
H = 5376
PART = 672
FULL = 640
REM = PART - FULL
NY = 8
SOURCES = 16
TOKENS = SOURCES * 24
PAIRS = SOURCES // 2
PAIR_ROWS = 256
VOCAB_LOCAL = 256
PIECE = VOCAB_LOCAL // 2
WORDS = 4 * VOCAB_LOCAL
SMALL = pltpu.CompilerParams(vmem_limit_bytes=8 * 1024 * 1024)


def loss_kernel(*refs):
    g_any, blocks = refs[0], refs[1:5]
    gain_ref, target_ref, place_ref, out_ref, g, e, xn, logits, g_sem, e_sem = refs[5:]

    def g_copy(pair):
        rows = pl.ds(pl.multiple_of(pair * PAIR_ROWS, PAIR_ROWS), PAIR_ROWS)
        return pltpu.make_async_copy(g_any.at[:, rows, :], g.at[:, rows, :], g_sem.at[pair])

    for pair in range(PAIRS):
        g_copy(pair).start()
    e_copies = [
        pltpu.make_async_copy(block, e.at[i * VOCAB_LOCAL : (i + 1) * VOCAB_LOCAL, :], e_sem.at[i])
        for i, block in enumerate(blocks)
    ]
    for copy in e_copies:
        copy.start()
    lane = lax.broadcasted_iota(jnp.int32, (16, 128), 1)

    def pair_step(pair, carry):
        g_copy(pair).wait()
        base = pair * PAIR_ROWS

        def tile(y, row):
            rows = pl.ds(pl.multiple_of(base + row, 16), 16)
            return g[y, rows, :].astype(jnp.float32)

        rest = [tile(y, 240) for y in range(NY)]
        for group in range(3):
            last = []
            for half in range(2):
                joined = None
                for q in range(4):
                    moved = rest[half * 4 + q]
                    shift = (q - group) * 32 % 128
                    if shift:
                        moved = pltpu.roll(moved, shift, 1)
                    joined = moved if joined is None else jnp.where(lane >= q * 32, moved, joined)
                last.append(joined)
            square = last[0] * last[0] + last[1] * last[1]
            for y in range(NY):
                for j in range(5):
                    value = tile(y, j * 48 + group * 16)
                    square = square + value * value
            scale = lax.rsqrt(jnp.sum(square, axis=1, keepdims=True) / H + epsilon)
            rows = pl.ds(pl.multiple_of(pair * 48 + group * 16, 16), 16)
            for y in range(NY):
                for j in range(5):
                    k = (y * 5 + j) * 128
                    value = tile(y, j * 48 + group * 16)
                    xn[rows, k : k + 128] = (value * scale * gain_ref[0:1, k : k + 128]).astype(jnp.bfloat16)
            for half in range(2):
                k = NY * FULL + half * 128
                xn[rows, k : k + 128] = (last[half] * scale * gain_ref[0:1, k : k + 128]).astype(jnp.bfloat16)
        return carry

    lax.fori_loop(0, PAIRS, pair_step, 0)

    for words, arrivals in ((slice(0, WORDS // 2), e_copies[:2]), (slice(WORDS // 2, WORDS), e_copies[2:])):
        for copy in arrivals:
            copy.wait()
        logits[:, words] = lax.dot_general(
            xn[...], e[words, :], (((1,), (1,)), ((), ())), preferred_element_type=jnp.float32
        )

    lane = lax.broadcasted_iota(jnp.int32, (48, 128), 1)
    stats = []
    for step in range(TOKENS // 48):
        rows = pl.ds(step * 48, 48)
        parts = [logits[rows, i * 128 : (i + 1) * 128] for i in range(WORDS // 128)]
        peak = parts[0]
        for part in parts[1:]:
            peak = jnp.maximum(peak, part)
        peak = jnp.max(peak, axis=1, keepdims=True)
        target = target_ref[rows, :]
        total = jnp.zeros((48, 128), jnp.float32)
        picked = jnp.zeros((48, 128), jnp.float32)
        for i, part in enumerate(parts):
            total = total + jnp.exp(part - peak)
            picked = picked + jnp.where(target - place_ref[i] == lane, part, 0.0)
        total = jnp.sum(total, axis=1, keepdims=True)
        picked = jnp.sum(picked, axis=1, keepdims=True)
        stats.append(jnp.where(lane == 0, peak, jnp.where(lane == 1, total, picked)))
    stats = jnp.concatenate(stats, axis=0)
    for i in range(TOKENS // 128):
        out_ref[:, i * 128 : (i + 1) * 128] = stats[i * 128 : (i + 1) * 128, :].T[0:8, :]


def local_losses(gathered, blocks, gain, target, place):
    any_space = pl.BlockSpec(memory_space=pl.ANY)
    vmem = pl.BlockSpec(memory_space=pltpu.VMEM)
    gathered = pltpu.with_memory_space_constraint(gathered, pltpu.HBM)
    blocks = [pltpu.with_memory_space_constraint(a, pltpu.VMEM) for a in blocks]
    return pl.pallas_call(
        loss_kernel,
        out_shape=jax.ShapeDtypeStruct((8, TOKENS), jnp.float32),
        in_specs=[any_space] * 5 + [vmem, vmem,  pl.BlockSpec(memory_space=pltpu.SMEM)],
        out_specs=vmem,
        scratch_shapes=[
            pltpu.VMEM((NY, PAIRS * PAIR_ROWS, 128), jnp.bfloat16),
            pltpu.VMEM((WORDS, H), jnp.bfloat16),
            pltpu.VMEM((TOKENS, H), jnp.bfloat16),
            pltpu.VMEM((TOKENS, WORDS), jnp.float32),
            pltpu.SemaphoreType.DMA((PAIRS,)),
            pltpu.SemaphoreType.DMA((len(blocks),)),
        ],
        compiler_params=pltpu.CompilerParams(vmem_limit_bytes=24 * 1024 * 1024),
        cost_estimate=pl.CostEstimate(flops=2 * TOKENS * WORDS * H, bytes_accessed=16 * 1024 * 1024, transcendentals=TOKENS * WORDS),
    )(gathered, *blocks, gain, target, place)


def prepare_kernel(hidden_ref, targets_ref, out_ref):
    row = lax.broadcasted_iota(jnp.int32, (24, 24), 0)
    column = lax.broadcasted_iota(jnp.int32, (24, 24), 1)
    lane = lax.broadcasted_iota(jnp.int32, (24, 128), 1)
    for m in range(2):
        target = jnp.sum(jnp.where(row == column, targets_ref[m : m + 1, :], 0), axis=1, keepdims=True)
        digits = jnp.where(lane == 80, target & 127, jnp.where(lane == 81, (target >> 7) & 127, target >> 14))
        first, second = (hidden_ref[m, :, k : k + 128].astype(jnp.float32) for k in (0, 128))
        tail = jnp.pad(hidden_ref[m, :, 256:336].astype(jnp.float32), ((0, 0), (0, 48)))
        tail = jnp.where(lane < 80, tail, digits.astype(jnp.float32))
        fold = jnp.concatenate([pltpu.roll(tail[16:24], 83, 1), pltpu.roll(tail[16:24], 41, 1)], axis=0)
        parts = [first[0:16], second[0:16], jnp.concatenate([first[16:24], second[16:24]], axis=0)]
        parts.append(jnp.where(lane[0:16] < 83, tail[0:16], fold))
        for i, part in enumerate(parts):
            part = part.astype(jnp.bfloat16)
            for s in range(SOURCES):
                out_ref[2 * s + m, i * 16 : (i + 1) * 16, :] = part


def prepare(hidden, targets):
    hidden, targets = (pltpu.with_memory_space_constraint(a, pltpu.HBM) for a in (hidden, targets))
    return pl.pallas_call(
        prepare_kernel,
        out_shape=jax.ShapeDtypeStruct((2 * SOURCES, 64, 128), jnp.bfloat16),
        compiler_params=SMALL,
    )(hidden, targets)


def repack_kernel(got_ref, units_ref, target_ref):
    lane = lax.broadcasted_iota(jnp.int32, (48, 128), 1)
    short = lane[0:16]
    weight = jnp.where(lane == 80, 1, jnp.where(lane == 81, 128, jnp.where(lane == 82, 16384, 0))).astype(jnp.float32)

    def pair_step(pair, carry):
        def rows_of(c):
            whole, tails = ([], []), []
            for d in range(2):
                block = [got_ref[4 * pair + 2 * d + c, i * 16 : (i + 1) * 16, :].astype(jnp.float32) for i in range(4)]
                whole[0].extend([block[0], block[2][0:8]])
                whole[1].extend([block[1], block[2][8:16]])
                fold = block[3]
                unfolded = jnp.where(short[0:8] < 42, pltpu.roll(fold[0:8], 45, 1), pltpu.roll(fold[8:16], 87, 1))
                tails.extend([fold, unfolded])
            return [jnp.concatenate(part, axis=0) for part in (*whole, tails)]

        (a0, a1, a), (b0, b1, b) = rows_of(0), rows_of(1)
        tiles = [a0, a1, b0, b1, jnp.where(lane < 80, a, pltpu.roll(b, 80, 1))]
        base = pair * PAIR_ROWS
        for j in range(5):
            rows = pl.ds(pl.multiple_of(base + j * 48, 16), 48)
            units_ref[rows, :] = tiles[j].astype(jnp.bfloat16)
        rest = [pltpu.roll(b[g * 16 : (g + 1) * 16], (32 * g - 48) % 128, 1) for g in range(3)]
        rest = jnp.where(short < 32, rest[0], jnp.where(short < 64, rest[1], jnp.where(short < 96, rest[2], 0.0)))
        units_ref[pl.ds(pl.multiple_of(base + 240, 16), 16), :] = rest.astype(jnp.bfloat16)
        target = jnp.sum(a * weight, axis=1, keepdims=True)
        target_ref[pl.ds(pl.multiple_of(pair * 48, 16), 48), :] = target.astype(jnp.int32)
        return carry

    lax.fori_loop(0, PAIRS, pair_step, 0)


def repack(got):
    return pl.pallas_call(
        repack_kernel,
        out_shape=(
            pltpu.HBM((PAIRS * PAIR_ROWS, 128), jnp.bfloat16),
            jax.ShapeDtypeStruct((TOKENS, 1), jnp.int32),
        ),
        compiler_params=SMALL,
        cost_estimate=pl.CostEstimate(flops=2000000, bytes_accessed=1200000, transcendentals=0),
    )(got)


def pieces():
    for y in range(NY):
        for begin, end in ((0, 256), (336, 592), (256, 336), (592, 640)):
            yield y * PART + begin, y * PART + end
    for y in range(NY):
        yield y * PART + FULL, (y + 1) * PART


def arrange(tiles, lane):
    def window(begin):
        k, shift = divmod(begin, 128)
        if shift == 0:
            return tiles[k]
        after = pltpu.roll(tiles[(k + 1) % len(tiles)], 128 - shift, 1)
        return jnp.where(lane < 128 - shift, pltpu.roll(tiles[k], 128 - shift, 1), after)

    out = []
    for y in range(NY):
        at = y * PART
        out += [window(at), window(at + 128), window(at + 336), window(at + 464)]
        out.append(jnp.where(lane < 80, window(at + 256), window(at + 592 - 80)))
    for half in range(2):
        joined = None
        for q in range(4):
            k, shift = divmod((half * 4 + q) * PART + FULL, 128)
            moved = tiles[k]
            if (q * 32 - shift) % 128:
                moved = pltpu.roll(moved, (q * 32 - shift) % 128, 1)
            joined = moved if joined is None else jnp.where(lane >= q * 32, moved, joined)
        out.append(joined)
    return out


def arrange_gain_kernel(gain_ref, out_ref):
    lane = lax.broadcasted_iota(jnp.int32, (8, 128), 1)
    tiles = [jnp.broadcast_to(gain_ref[:, k * 128 : (k + 1) * 128], (8, 128)) for k in range(H // 128)]
    for k, tile in enumerate(arrange(tiles, lane)):
        out_ref[:, k * 128 : (k + 1) * 128] = tile


def arrange_gain(gain):
    return pl.pallas_call(
        arrange_gain_kernel, out_shape=jax.ShapeDtypeStruct((8, H), jnp.float32), compiler_params=SMALL
    )(gain.reshape(1, H))


def reorder_kernel(ref, out_ref, *piece_refs):
    lane = lax.broadcasted_iota(jnp.int32, (16, 128), 1)
    for n, piece_ref in enumerate(piece_refs):

        def step(i, carry):
            src = pl.ds(pl.multiple_of(n * PIECE + i * 16, 16), 16)
            dst = pl.ds(pl.multiple_of(i * 16, 16), 16)
            tiles = [ref[src, k * 128 : (k + 1) * 128].astype(jnp.float32) for k in range(H // 128)]
            for k, tile in enumerate(arrange(tiles, lane)):
                columns = slice(k * 128, (k + 1) * 128)
                out_ref[src, columns] = piece_ref[dst, columns] = tile.astype(jnp.bfloat16)
            return carry

        lax.fori_loop(0, PIECE // 16, step, 0)


def reorder_rows(rows):
    piece = jax.ShapeDtypeStruct((PIECE, H), jnp.bfloat16)
    return pl.pallas_call(
        reorder_kernel,
        out_shape=(jax.ShapeDtypeStruct((VOCAB_LOCAL, H), jnp.bfloat16), piece, piece),
        compiler_params=pltpu.CompilerParams(vmem_limit_bytes=16 * 1024 * 1024),
        cost_estimate=pl.CostEstimate(flops=VOCAB_LOCAL * H * 8, bytes_accessed=VOCAB_LOCAL * H * 4, transcendentals=0),
    )(rows)


def combine(peak, total, picked, axis):
    top = jnp.max(peak, axis=axis)
    total = jnp.sum(total * jnp.exp(peak - jnp.expand_dims(top, axis)), axis=axis)
    return top, total, jnp.sum(picked, axis=axis)


def per_device(hidden, norm_gain, embedding, targets):
    swap = [(0, 1), (1, 0)]
    tie = lax.optimization_barrier
    xh, xl, z, y, core = (lax.axis_index(a) for a in ("xh", "xl", "z", "y", "core"))

    x = xh * 2 + xl

    def first_row(at, c):
        return (((at % 4 * 8 + z) * 8 + y) * 2 + c) * VOCAB_LOCAL

    near = [first_row(x, c) + n * PIECE for c in (core, 1 - core) for n in range(2)]
    far = [first_row(x + 3 - 2 * n, c) + n * PIECE for c in (core, 1 - core) for n in range(2)]
    place = jnp.stack(near + far)

    payload, embedding = tie((prepare(hidden, targets), embedding))
    got = lax.all_to_all(payload, ("xh", "z", "core"), 0, 0, tiled=True)
    units, target = repack(got)

    units, late, gain = tie((units, embedding, norm_gain))
    gathered = lax.all_gather(units, "y", axis=0)

    own, low, high = reorder_rows(late)
    from_left = lax.ppermute(low, ("xh", "xl"), [(i, (i + 1) % 4) for i in range(4)])
    from_right = lax.ppermute(high, ("xh", "xl"), [(i, (i - 1) % 4) for i in range(4)])
    beside = lax.ppermute(own, "core", swap)
    far = jnp.concatenate([from_left, from_right], axis=0)
    far_beside = lax.ppermute(far, "core", swap)
    stats = local_losses(gathered, (own, beside, far, far_beside), arrange_gain(gain), target, place)
    stats = stats[:3].reshape(3, SOURCES, 24).transpose(1, 0, 2)
    stats = lax.all_to_all(stats, ("xh", "z"), 0, 0, tiled=True)
    part = jnp.stack(combine(stats[:, 0], stats[:, 1], stats[:, 2], 0))
    every = lax.all_to_all(jnp.broadcast_to(part[None], (16, 3, 24)), ("y", "core"), 0, 0, tiled=True)
    every = every.reshape(NY, 2, 3, 24)
    peak, total, picked = combine(every[:, :, 0], every[:, :, 1], every[:, :, 2], 0)
    return peak + jnp.log(total) - picked


def solution(mesh):
    fine = Mesh(mesh.devices.reshape(2, 2, 8, 8, 2), ("xh", "xl", "z", "y", "core"))
    dp, pipe = ("xh", "xl", "z"), ("y", "core")
    placed = (P(None, dp, pipe), P(), P(dp + pipe, None), P(None, dp))
    return jax.shard_map(per_device, mesh=fine, in_specs=placed, out_specs=P(None, dp), check_vma=False)
```

```python
import jax
import jax.numpy as jnp
import numpy as np
from jax import lax
from jax.experimental import pallas as pl
from jax.experimental.pallas import tpu as pltpu
from jax.sharding import Mesh
from jax.sharding import PartitionSpec as P

epsilon = 1e-06
H = 5376
PART = 672
FULL = 640
REM = PART - FULL
NY = 8
SOURCES = 16
TOKENS = SOURCES * 24
PAIRS = SOURCES // 2
PAIR_ROWS = 256
VOCAB_LOCAL = 256
PIECE = VOCAB_LOCAL // 2
WORDS = 4 * VOCAB_LOCAL
SMALL = pltpu.CompilerParams(vmem_limit_bytes=8 * 1024 * 1024)


def loss_kernel(*refs):
    g_any, blocks = refs[0], refs[1:5]
    gain_ref, target_ref, place_ref, out_ref, g, e, xn, logits, g_sem, e_sem = refs[5:]

    def g_copy(pair):
        rows = pl.ds(pl.multiple_of(pair * PAIR_ROWS, PAIR_ROWS), PAIR_ROWS)
        return pltpu.make_async_copy(g_any.at[:, rows, :], g.at[:, rows, :], g_sem.at[pair])

    for pair in range(PAIRS):
        g_copy(pair).start()
    e_copies = [
        pltpu.make_async_copy(block, e.at[i * VOCAB_LOCAL : (i + 1) * VOCAB_LOCAL, :], e_sem.at[i])
        for i, block in enumerate(blocks)
    ]
    for copy in e_copies:
        copy.start()
    lane = lax.broadcasted_iota(jnp.int32, (16, 128), 1)

    def pair_step(pair, carry):
        g_copy(pair).wait()
        base = pair * PAIR_ROWS

        def tile(y, row):
            rows = pl.ds(pl.multiple_of(base + row, 16), 16)
            return g[y, rows, :].astype(jnp.float32)

        rest = [tile(y, 240) for y in range(NY)]
        for group in range(3):
            last = []
            for half in range(2):
                joined = None
                for q in range(4):
                    moved = rest[half * 4 + q]
                    shift = (q - group) * 32 % 128
                    if shift:
                        moved = pltpu.roll(moved, shift, 1)
                    joined = moved if joined is None else jnp.where(lane >= q * 32, moved, joined)
                last.append(joined)
            square = last[0] * last[0] + last[1] * last[1]
            for y in range(NY):
                for j in range(5):
                    value = tile(y, j * 48 + group * 16)
                    square = square + value * value
            scale = lax.rsqrt(jnp.sum(square, axis=1, keepdims=True) / H + epsilon)
            rows = pl.ds(pl.multiple_of(pair * 48 + group * 16, 16), 16)
            for y in range(NY):
                for j in range(5):
                    k = (y * 5 + j) * 128
                    value = tile(y, j * 48 + group * 16)
                    xn[rows, k : k + 128] = (value * scale * gain_ref[0:1, k : k + 128]).astype(jnp.bfloat16)
            for half in range(2):
                k = NY * FULL + half * 128
                xn[rows, k : k + 128] = (last[half] * scale * gain_ref[0:1, k : k + 128]).astype(jnp.bfloat16)
        return carry

    lax.fori_loop(0, PAIRS, pair_step, 0)

    for words, arrivals in ((slice(0, WORDS // 2), e_copies[:2]), (slice(WORDS // 2, WORDS), e_copies[2:])):
        for copy in arrivals:
            copy.wait()
        logits[:, words] = lax.dot_general(
            xn[...], e[words, :], (((1,), (1,)), ((), ())), preferred_element_type=jnp.float32
        )

    lane = lax.broadcasted_iota(jnp.int32, (48, 128), 1)
    stats = []
    for step in range(TOKENS // 48):
        rows = pl.ds(step * 48, 48)
        parts = [logits[rows, i * 128 : (i + 1) * 128] for i in range(WORDS // 128)]
        peak = parts[0]
        for part in parts[1:]:
            peak = jnp.maximum(peak, part)
        peak = jnp.max(peak, axis=1, keepdims=True)
        target = target_ref[rows, :]
        total = jnp.zeros((48, 128), jnp.float32)
        picked = jnp.zeros((48, 128), jnp.float32)
        for i, part in enumerate(parts):
            total = total + jnp.exp(part - peak)
            picked = picked + jnp.where(target - place_ref[i] == lane, part, 0.0)
        total = jnp.sum(total, axis=1, keepdims=True)
        picked = jnp.sum(picked, axis=1, keepdims=True)
        stats.append(jnp.where(lane == 0, peak, jnp.where(lane == 1, total, picked)))
    stats = jnp.concatenate(stats, axis=0)
    for i in range(TOKENS // 128):
        out_ref[:, i * 128 : (i + 1) * 128] = stats[i * 128 : (i + 1) * 128, :].T[0:8, :]


def local_losses(gathered, blocks, gain, target, place):
    any_space = pl.BlockSpec(memory_space=pl.ANY)
    vmem = pl.BlockSpec(memory_space=pltpu.VMEM)
    gathered = pltpu.with_memory_space_constraint(gathered, pltpu.HBM)
    blocks = [pltpu.with_memory_space_constraint(a, pltpu.VMEM) for a in blocks]
    return pl.pallas_call(
        loss_kernel,
        out_shape=jax.ShapeDtypeStruct((8, TOKENS), jnp.float32),
        in_specs=[any_space] * 5 + [vmem, vmem,  pl.BlockSpec(memory_space=pltpu.SMEM)],
        out_specs=vmem,
        scratch_shapes=[
            pltpu.VMEM((NY, PAIRS * PAIR_ROWS, 128), jnp.bfloat16),
            pltpu.VMEM((WORDS, H), jnp.bfloat16),
            pltpu.VMEM((TOKENS, H), jnp.bfloat16),
            pltpu.VMEM((TOKENS, WORDS), jnp.float32),
            pltpu.SemaphoreType.DMA((PAIRS,)),
            pltpu.SemaphoreType.DMA((len(blocks),)),
        ],
        compiler_params=pltpu.CompilerParams(vmem_limit_bytes=24 * 1024 * 1024),
        cost_estimate=pl.CostEstimate(flops=2 * TOKENS * WORDS * H, bytes_accessed=16 * 1024 * 1024, transcendentals=TOKENS * WORDS),
    )(gathered, *blocks, gain, target, place)


def prepare_kernel(hidden_ref, targets_ref, out_ref):
    row = lax.broadcasted_iota(jnp.int32, (24, 24), 0)
    column = lax.broadcasted_iota(jnp.int32, (24, 24), 1)
    lane = lax.broadcasted_iota(jnp.int32, (24, 128), 1)
    for m in range(2):
        target = jnp.sum(jnp.where(row == column, targets_ref[m : m + 1, :], 0), axis=1, keepdims=True)
        digits = jnp.where(lane == 80, target & 127, jnp.where(lane == 81, (target >> 7) & 127, target >> 14))
        first, second = (hidden_ref[m, :, k : k + 128].astype(jnp.float32) for k in (0, 128))
        tail = jnp.pad(hidden_ref[m, :, 256:336].astype(jnp.float32), ((0, 0), (0, 48)))
        tail = jnp.where(lane < 80, tail, digits.astype(jnp.float32))
        fold = jnp.concatenate([pltpu.roll(tail[16:24], 83, 1), pltpu.roll(tail[16:24], 41, 1)], axis=0)
        parts = [first[0:16], second[0:16], jnp.concatenate([first[16:24], second[16:24]], axis=0)]
        parts.append(jnp.where(lane[0:16] < 83, tail[0:16], fold))
        for i, part in enumerate(parts):
            part = part.astype(jnp.bfloat16)
            for s in range(SOURCES):
                out_ref[2 * s + m, i * 16 : (i + 1) * 16, :] = part


def prepare(hidden, targets):
    hidden, targets = (pltpu.with_memory_space_constraint(a, pltpu.HBM) for a in (hidden, targets))
    return pl.pallas_call(
        prepare_kernel,
        out_shape=jax.ShapeDtypeStruct((2 * SOURCES, 64, 128), jnp.bfloat16),
        compiler_params=SMALL,
    )(hidden, targets)


def repack_kernel(got_ref, units_ref, target_ref):
    lane = lax.broadcasted_iota(jnp.int32, (48, 128), 1)
    short = lane[0:16]
    weight = jnp.where(lane == 80, 1, jnp.where(lane == 81, 128, jnp.where(lane == 82, 16384, 0))).astype(jnp.float32)

    def pair_step(pair, carry):
        def rows_of(c):
            whole, tails = ([], []), []
            for d in range(2):
                block = [got_ref[4 * pair + 2 * d + c, i * 16 : (i + 1) * 16, :].astype(jnp.float32) for i in range(4)]
                whole[0].extend([block[0], block[2][0:8]])
                whole[1].extend([block[1], block[2][8:16]])
                fold = block[3]
                unfolded = jnp.where(short[0:8] < 42, pltpu.roll(fold[0:8], 45, 1), pltpu.roll(fold[8:16], 87, 1))
                tails.extend([fold, unfolded])
            return [jnp.concatenate(part, axis=0) for part in (*whole, tails)]

        (a0, a1, a), (b0, b1, b) = rows_of(0), rows_of(1)
        tiles = [a0, a1, b0, b1, jnp.where(lane < 80, a, pltpu.roll(b, 80, 1))]
        base = pair * PAIR_ROWS
        for j in range(5):
            rows = pl.ds(pl.multiple_of(base + j * 48, 16), 48)
            units_ref[rows, :] = tiles[j].astype(jnp.bfloat16)
        rest = [pltpu.roll(b[g * 16 : (g + 1) * 16], (32 * g - 48) % 128, 1) for g in range(3)]
        rest = jnp.where(short < 32, rest[0], jnp.where(short < 64, rest[1], jnp.where(short < 96, rest[2], 0.0)))
        units_ref[pl.ds(pl.multiple_of(base + 240, 16), 16), :] = rest.astype(jnp.bfloat16)
        target = jnp.sum(a * weight, axis=1, keepdims=True)
        target_ref[pl.ds(pl.multiple_of(pair * 48, 16), 48), :] = target.astype(jnp.int32)
        return carry

    lax.fori_loop(0, PAIRS, pair_step, 0, unroll=True)


def repack(got):
    return pl.pallas_call(
        repack_kernel,
        out_shape=(
            pltpu.HBM((PAIRS * PAIR_ROWS, 128), jnp.bfloat16),
            jax.ShapeDtypeStruct((TOKENS, 1), jnp.int32),
        ),
        compiler_params=SMALL,
        cost_estimate=pl.CostEstimate(flops=2000000, bytes_accessed=1200000, transcendentals=0),
    )(got)


def pieces():
    for y in range(NY):
        for begin, end in ((0, 256), (336, 592), (256, 336), (592, 640)):
            yield y * PART + begin, y * PART + end
    for y in range(NY):
        yield y * PART + FULL, (y + 1) * PART


def arrange(tiles, lane):
    def window(begin):
        k, shift = divmod(begin, 128)
        if shift == 0:
            return tiles[k]
        after = pltpu.roll(tiles[(k + 1) % len(tiles)], 128 - shift, 1)
        return jnp.where(lane < 128 - shift, pltpu.roll(tiles[k], 128 - shift, 1), after)

    out = []
    for y in range(NY):
        at = y * PART
        out += [window(at), window(at + 128), window(at + 336), window(at + 464)]
        out.append(jnp.where(lane < 80, window(at + 256), window(at + 592 - 80)))
    for half in range(2):
        joined = None
        for q in range(4):
            k, shift = divmod((half * 4 + q) * PART + FULL, 128)
            moved = tiles[k]
            if (q * 32 - shift) % 128:
                moved = pltpu.roll(moved, (q * 32 - shift) % 128, 1)
            joined = moved if joined is None else jnp.where(lane >= q * 32, moved, joined)
        out.append(joined)
    return out


def arrange_gain_kernel(gain_ref, out_ref):
    lane = lax.broadcasted_iota(jnp.int32, (8, 128), 1)
    tiles = [jnp.broadcast_to(gain_ref[:, k * 128 : (k + 1) * 128], (8, 128)) for k in range(H // 128)]
    for k, tile in enumerate(arrange(tiles, lane)):
        out_ref[:, k * 128 : (k + 1) * 128] = tile


def arrange_gain(gain):
    return pl.pallas_call(
        arrange_gain_kernel, out_shape=jax.ShapeDtypeStruct((8, H), jnp.float32), compiler_params=SMALL
    )(gain.reshape(1, H))


def reorder_kernel(ref, out_ref, *piece_refs):
    lane = lax.broadcasted_iota(jnp.int32, (16, 128), 1)
    for n, piece_ref in enumerate(piece_refs):

        def step(i, carry):
            src = pl.ds(pl.multiple_of(n * PIECE + i * 16, 16), 16)
            dst = pl.ds(pl.multiple_of(i * 16, 16), 16)
            tiles = [ref[src, k * 128 : (k + 1) * 128].astype(jnp.float32) for k in range(H // 128)]
            for k, tile in enumerate(arrange(tiles, lane)):
                columns = slice(k * 128, (k + 1) * 128)
                out_ref[src, columns] = piece_ref[dst, columns] = tile.astype(jnp.bfloat16)
            return carry

        lax.fori_loop(0, PIECE // 16, step, 0)


def reorder_rows(rows):
    piece = jax.ShapeDtypeStruct((PIECE, H), jnp.bfloat16)
    return pl.pallas_call(
        reorder_kernel,
        out_shape=(jax.ShapeDtypeStruct((VOCAB_LOCAL, H), jnp.bfloat16), piece, piece),
        compiler_params=pltpu.CompilerParams(vmem_limit_bytes=16 * 1024 * 1024),
        cost_estimate=pl.CostEstimate(flops=VOCAB_LOCAL * H * 8, bytes_accessed=VOCAB_LOCAL * H * 4, transcendentals=0),
    )(rows)


def combine(peak, total, picked, axis):
    top = jnp.max(peak, axis=axis)
    total = jnp.sum(total * jnp.exp(peak - jnp.expand_dims(top, axis)), axis=axis)
    return top, total, jnp.sum(picked, axis=axis)


def per_device(hidden, norm_gain, embedding, targets):
    swap = [(0, 1), (1, 0)]
    tie = lax.optimization_barrier
    xh, xl, z, y, core = (lax.axis_index(a) for a in ("xh", "xl", "z", "y", "core"))

    x = xh * 2 + xl

    def first_row(at, c):
        return (((at % 4 * 8 + z) * 8 + y) * 2 + c) * VOCAB_LOCAL

    near = [first_row(x, c) + n * PIECE for c in (core, 1 - core) for n in range(2)]
    far = [first_row(x + 3 - 2 * n, c) + n * PIECE for c in (core, 1 - core) for n in range(2)]
    place = jnp.stack(near + far)

    payload, embedding = tie((prepare(hidden, targets), embedding))
    got = lax.all_to_all(payload, ("xh", "z", "core"), 0, 0, tiled=True)
    units, target = repack(got)

    units, late, gain = tie((units, embedding, norm_gain))
    gathered = lax.all_gather(units, "y", axis=0)

    own, low, high = reorder_rows(late)
    from_left = lax.ppermute(low, ("xh", "xl"), [(i, (i + 1) % 4) for i in range(4)])
    from_right = lax.ppermute(high, ("xh", "xl"), [(i, (i - 1) % 4) for i in range(4)])
    beside = lax.ppermute(own, "core", swap)
    far = jnp.concatenate([from_left, from_right], axis=0)
    far_beside = lax.ppermute(far, "core", swap)
    stats = local_losses(gathered, (own, beside, far, far_beside), arrange_gain(gain), target, place)
    stats = stats[:3].reshape(3, SOURCES, 24).transpose(1, 0, 2)
    stats = lax.all_to_all(stats, ("xh", "z"), 0, 0, tiled=True)
    part = jnp.stack(combine(stats[:, 0], stats[:, 1], stats[:, 2], 0))
    every = lax.all_to_all(jnp.broadcast_to(part[None], (16, 3, 24)), ("y", "core"), 0, 0, tiled=True)
    every = every.reshape(NY, 2, 3, 24)
    peak, total, picked = combine(every[:, :, 0], every[:, :, 1], every[:, :, 2], 0)
    return peak + jnp.log(total) - picked


def solution(mesh):
    fine = Mesh(mesh.devices.reshape(2, 2, 8, 8, 2), ("xh", "xl", "z", "y", "core"))
    dp, pipe = ("xh", "xl", "z"), ("y", "core")
    placed = (P(None, dp, pipe), P(), P(dp + pipe, None), P(None, dp))
    return jax.shard_map(per_device, mesh=fine, in_specs=placed, out_specs=P(None, dp), check_vma=False)
```

```python
import jax
import jax.numpy as jnp
import numpy as np
from jax import lax
from jax.experimental import pallas as pl
from jax.experimental.pallas import tpu as pltpu
from jax.sharding import Mesh
from jax.sharding import PartitionSpec as P

epsilon = 1e-06
H = 5376
PART = 336
PARTS = H // PART
SOURCES = 16
TOKENS = SOURCES * 24
OWN = 48
VOCAB_LOCAL = 256
WORDS = 4 * VOCAB_LOCAL
SMALL = pltpu.CompilerParams(vmem_limit_bytes=8 * 1024 * 1024)
PIECE = VOCAB_LOCAL // 2


def loss_kernel(*refs):
    rows_any, blocks = refs[0], refs[1:5]
    target_ref, place_ref, out_ref, xn, e, logits, x_sem, e_sem = refs[5:]
    x_copies = []
    for n in range(TOKENS // 96):
        rows = slice(n * 96, (n + 1) * 96)
        x_copies.append(pltpu.make_async_copy(rows_any.at[rows, :], xn.at[rows, :], x_sem.at[n]))
    e_copies = []
    for i, block in enumerate(blocks):
        words = slice(i * VOCAB_LOCAL, (i + 1) * VOCAB_LOCAL)
        e_copies.append(pltpu.make_async_copy(block, e.at[words, :], e_sem.at[i]))
    for copy in x_copies + e_copies:
        copy.start()
    for words, arrivals in ((slice(0, WORDS // 2), x_copies + e_copies[:2]), (slice(WORDS // 2, WORDS), e_copies[2:])):
        for copy in arrivals:
            copy.wait()
        logits[:, words] = lax.dot_general(
            xn[...], e[words, :], (((1,), (1,)), ((), ())), preferred_element_type=jnp.float32
        )

    lane = lax.broadcasted_iota(jnp.int32, (48, 128), 1)
    stats = []
    for step in range(TOKENS // 48):
        rows = pl.ds(step * 48, 48)
        parts = [logits[rows, i * 128 : (i + 1) * 128] for i in range(WORDS // 128)]
        peak = parts[0]
        for part in parts[1:]:
            peak = jnp.maximum(peak, part)
        peak = jnp.max(peak, axis=1, keepdims=True)
        target = target_ref[rows, :]
        total = jnp.zeros((48, 128), jnp.float32)
        picked = jnp.zeros((48, 128), jnp.float32)
        for i, part in enumerate(parts):
            total = total + jnp.exp(part - peak)
            picked = picked + jnp.where(target - place_ref[i] == lane, part, 0.0)
        total = jnp.sum(total, axis=1, keepdims=True)
        picked = jnp.sum(picked, axis=1, keepdims=True)
        stats.append(jnp.where(lane == 0, peak, jnp.where(lane == 1, total, picked)))
    stats = jnp.concatenate(stats, axis=0)
    for i in range(TOKENS // 128):
        out_ref[:, i * 128 : (i + 1) * 128] = stats[i * 128 : (i + 1) * 128, :].T[0:8, :]


def local_losses(rows, blocks, target, place):
    any_space = pl.BlockSpec(memory_space=pl.ANY)
    vmem = pl.BlockSpec(memory_space=pltpu.VMEM)
    rows = pltpu.with_memory_space_constraint(rows, pltpu.HBM)
    blocks = [pltpu.with_memory_space_constraint(a, pltpu.VMEM) for a in blocks]
    return pl.pallas_call(
        loss_kernel,
        out_shape=jax.ShapeDtypeStruct((8, TOKENS), jnp.float32),
        in_specs=[any_space] * 5 + [vmem, pl.BlockSpec(memory_space=pltpu.SMEM)],
        out_specs=vmem,
        scratch_shapes=[
            pltpu.VMEM((TOKENS, H), jnp.bfloat16),
            pltpu.VMEM((WORDS, H), jnp.bfloat16),
            pltpu.VMEM((TOKENS, WORDS), jnp.float32),
            pltpu.SemaphoreType.DMA((TOKENS // 96,)),
            pltpu.SemaphoreType.DMA((len(blocks),)),
        ],
        compiler_params=pltpu.CompilerParams(vmem_limit_bytes=24 * 1024 * 1024),
        cost_estimate=pl.CostEstimate(flops=2 * TOKENS * WORDS * H, bytes_accessed=16 * 1024 * 1024, transcendentals=TOKENS * WORDS),
    )(rows, *blocks, target, place)


def prepare_kernel(hidden_ref, out_ref):
    lane = lax.broadcasted_iota(jnp.int32, (16, 128), 1)
    for m in range(2):
        first, second = (hidden_ref[m, :, k : k + 128].astype(jnp.float32) for k in (0, 128))
        tail = jnp.pad(hidden_ref[m, :, 256:336].astype(jnp.float32), ((0, 0), (0, 48)))
        fold = jnp.concatenate([pltpu.roll(tail[16:24], 80, 1), pltpu.roll(tail[16:24], 40, 1)], axis=0)
        parts = [first[0:16], second[0:16], jnp.concatenate([first[16:24], second[16:24]], axis=0)]
        parts.append(jnp.where(lane < 80, tail[0:16], fold))
        for i, part in enumerate(parts):
            part = part.astype(jnp.bfloat16)
            for s in range(SOURCES):
                out_ref[2 * s + m, i * 16 : (i + 1) * 16, :] = part


def prepare(hidden):
    return pl.pallas_call(
        prepare_kernel,
        out_shape=jax.ShapeDtypeStruct((2 * SOURCES, 64, 128), jnp.bfloat16),
        compiler_params=SMALL,
    )(pltpu.with_memory_space_constraint(hidden, pltpu.HBM))


def normalize_kernel(got_ref, gain_any, out_ref, rows_ref, gain_ref, gain_sem):
    gain_copy = pltpu.make_async_copy(gain_any, gain_ref, gain_sem)
    gain_copy.start()
    lane = lax.broadcasted_iota(jnp.int32, (24, 128), 1)
    scales = []
    for d in range(2):
        tiles = []
        for p in range(PARTS):
            block = [got_ref[d * PARTS + p, i * 16 : (i + 1) * 16, :].astype(jnp.float32) for i in range(4)]
            fold = block[3]
            unfolded = jnp.where(lane[0:8] < 40, pltpu.roll(fold[0:8], 48, 1), pltpu.roll(fold[8:16], 88, 1))
            whole = [(block[0], block[2][0:8]), (block[1], block[2][8:16]), (fold, unfolded)]
            tiles += [(p * PART + k * 128, jnp.concatenate(pair, axis=0)) for k, pair in enumerate(whole)]
        square = jnp.zeros((24, 128), jnp.float32)
        for t in range(H // 128):
            joined = None
            for begin, tile in tiles:
                width = 128 if begin % PART < 256 else 80
                at = begin - t * 128
                if at + width <= 0 or at >= 128:
                    continue
                moved = pltpu.roll(tile, at % 128, 1) if at % 128 else tile
                joined = moved if joined is None else jnp.where(lane >= at, moved, joined)
            rows_ref[d * 24 : (d + 1) * 24, t * 128 : (t + 1) * 128] = joined
            square = square + joined * joined
        scales.append(lax.rsqrt(jnp.sum(square, axis=1, keepdims=True) / H + epsilon))
    scale = jnp.concatenate(scales, axis=0)
    gain_copy.wait()
    for t in range(H // 128):
        columns = slice(t * 128, (t + 1) * 128)
        out_ref[:, columns] = (rows_ref[:, columns] * scale * gain_ref[columns].reshape(1, 128)).astype(jnp.bfloat16)


def normalize(got, gain):
    return pl.pallas_call(
        normalize_kernel,
        out_shape=pltpu.HBM((OWN, H), jnp.bfloat16),
        in_specs=[pl.BlockSpec(memory_space=pltpu.VMEM), pl.BlockSpec(memory_space=pl.ANY)],
        scratch_shapes=[pltpu.VMEM((OWN, H), jnp.float32), pltpu.VMEM((H,), jnp.float32), pltpu.SemaphoreType.DMA],
        compiler_params=SMALL,
        cost_estimate=pl.CostEstimate(flops=2000000, bytes_accessed=1200000, transcendentals=0),
    )(got, pltpu.with_memory_space_constraint(gain, pltpu.HBM))


def combine(peak, total, picked, axis):
    top = jnp.max(peak, axis=axis)
    total = jnp.sum(total * jnp.exp(peak - jnp.expand_dims(top, axis)), axis=axis)
    return top, total, jnp.sum(picked, axis=axis)


def per_device(hidden, norm_gain, embedding, targets):
    swap = [(0, 1), (1, 0)]
    tie = lax.optimization_barrier
    xh, xl, z, y, core = (lax.axis_index(a) for a in ("xh", "xl", "z", "y", "core"))

    x = xh * 2 + xl

    def first_row(at, c):
        return (((at % 4 * 8 + z) * 8 + y) * 2 + c) * VOCAB_LOCAL

    near = [first_row(x, c) + n * PIECE for c in (core, 1 - core) for n in range(2)]
    far = [first_row(x + 3 - 2 * n, c) + n * PIECE for c in (core, 1 - core) for n in range(2)]
    place = jnp.stack(near[:2] + far[:2] + near[2:] + far[2:])

    got = lax.all_to_all(prepare(hidden), ("xh", "y", "core"), 0, 0, tiled=True)
    normed = normalize(got, norm_gain)
    normed, late, asked = tie((normed, embedding, targets))
    rows = lax.all_gather(normed, "z", axis=0, tiled=True)

    from_left = lax.ppermute(late[:PIECE], ("xh", "xl"), [(i, (i + 1) % 4) for i in range(4)])
    from_right = lax.ppermute(late[PIECE:], ("xh", "xl"), [(i, (i - 1) % 4) for i in range(4)])
    beside = lax.ppermute(late, "core", swap)
    asked = jnp.broadcast_to(lax.dynamic_index_in_dim(asked, core, 0), (SOURCES, 24))
    target = lax.all_to_all(asked, ("z", "xh"), 0, 0, tiled=True).reshape(TOKENS, 1)
    from_left, from_right, target = tie((from_left, from_right, target))
    far = jnp.concatenate([from_left, from_right], axis=0)
    far_beside = lax.ppermute(far, "core", swap)
    stats = local_losses(rows, (late, far, beside, far_beside), target, place)
    stats = stats[:3].reshape(3, SOURCES, 24).transpose(1, 0, 2)
    stats = lax.all_to_all(stats, ("z", "xh"), 0, 0, tiled=True)
    part = jnp.stack(combine(stats[:, 0], stats[:, 1], stats[:, 2], 0))
    every = lax.all_to_all(jnp.broadcast_to(part[None], (16, 3, 24)), ("y", "core"), 0, 0, tiled=True)
    every = every.reshape(PARTS // 2, 2, 3, 24)
    peak, total, picked = combine(every[:, :, 0], every[:, :, 1], every[:, :, 2], 0)
    return peak + jnp.log(total) - picked


def solution(mesh):
    fine = Mesh(mesh.devices.reshape(2, 2, 8, 8, 2), ("xh", "xl", "z", "y", "core"))
    dp, pipe = ("xh", "xl", "z"), ("y", "core")
    placed = (P(None, dp, pipe), P(), P(dp + pipe, None), P(None, dp))
    return jax.shard_map(per_device, mesh=fine, in_specs=placed, out_specs=P(None, dp), check_vma=False)
```

```python
import jax
import jax.numpy as jnp
import numpy as np
from jax import lax
from jax.experimental import pallas as pl
from jax.experimental.pallas import tpu as pltpu
from jax.sharding import Mesh
from jax.sharding import PartitionSpec as P

epsilon = 1e-06
H = 5376
PART = 336
PARTS = H // PART
SOURCES = 16
TOKENS = SOURCES * 24
OWN = 48
VOCAB_LOCAL = 256
WORDS = 4 * VOCAB_LOCAL
SMALL = pltpu.CompilerParams(vmem_limit_bytes=8 * 1024 * 1024)
PIECE = VOCAB_LOCAL // 2


def loss_kernel(*refs):
    rows_any, blocks = refs[0], refs[1:7]
    target_ref, place_ref, out_ref, xn, e, logits, x_sem, e_sem = refs[7:]
    x_copies = []
    for n in range(TOKENS // 96):
        rows = slice(n * 96, (n + 1) * 96)
        x_copies.append(pltpu.make_async_copy(rows_any.at[rows, :], xn.at[rows, :], x_sem.at[n]))
    e_copies, begin = [], 0
    for i, block in enumerate(blocks):
        words = slice(begin, begin + block.shape[0])
        begin += block.shape[0]
        e_copies.append(pltpu.make_async_copy(block, e.at[words, :], e_sem.at[i]))
    for copy in x_copies + e_copies:
        copy.start()
    for words, arrivals in ((slice(0, WORDS // 2), x_copies + e_copies[:3]), (slice(WORDS // 2, WORDS), e_copies[3:])):
        for copy in arrivals:
            copy.wait()
        logits[:, words] = lax.dot_general(
            xn[...], e[words, :], (((1,), (1,)), ((), ())), preferred_element_type=jnp.float32
        )

    lane = lax.broadcasted_iota(jnp.int32, (48, 128), 1)
    stats = []
    for step in range(TOKENS // 48):
        rows = pl.ds(step * 48, 48)
        parts = [logits[rows, i * 128 : (i + 1) * 128] for i in range(WORDS // 128)]
        peak = parts[0]
        for part in parts[1:]:
            peak = jnp.maximum(peak, part)
        peak = jnp.max(peak, axis=1, keepdims=True)
        target = target_ref[rows, :]
        total = jnp.zeros((48, 128), jnp.float32)
        picked = jnp.zeros((48, 128), jnp.float32)
        for i, part in enumerate(parts):
            total = total + jnp.exp(part - peak)
            picked = picked + jnp.where(target - place_ref[i] == lane, part, 0.0)
        total = jnp.sum(total, axis=1, keepdims=True)
        picked = jnp.sum(picked, axis=1, keepdims=True)
        stats.append(jnp.where(lane == 0, peak, jnp.where(lane == 1, total, picked)))
    stats = jnp.concatenate(stats, axis=0)
    for i in range(TOKENS // 128):
        out_ref[:, i * 128 : (i + 1) * 128] = stats[i * 128 : (i + 1) * 128, :].T[0:8, :]


def local_losses(rows, blocks, target, place):
    any_space = pl.BlockSpec(memory_space=pl.ANY)
    vmem = pl.BlockSpec(memory_space=pltpu.VMEM)
    rows = pltpu.with_memory_space_constraint(rows, pltpu.HBM)
    blocks = [pltpu.with_memory_space_constraint(a, pltpu.VMEM) for a in blocks]
    return pl.pallas_call(
        loss_kernel,
        out_shape=jax.ShapeDtypeStruct((8, TOKENS), jnp.float32),
        in_specs=[any_space] * 7 + [vmem, pl.BlockSpec(memory_space=pltpu.SMEM)],
        out_specs=vmem,
        scratch_shapes=[
            pltpu.VMEM((TOKENS, H), jnp.bfloat16),
            pltpu.VMEM((WORDS, H), jnp.bfloat16),
            pltpu.VMEM((TOKENS, WORDS), jnp.float32),
            pltpu.SemaphoreType.DMA((TOKENS // 96,)),
            pltpu.SemaphoreType.DMA((len(blocks),)),
        ],
        compiler_params=pltpu.CompilerParams(vmem_limit_bytes=24 * 1024 * 1024),
        cost_estimate=pl.CostEstimate(flops=2 * TOKENS * WORDS * H, bytes_accessed=16 * 1024 * 1024, transcendentals=TOKENS * WORDS),
    )(rows, *blocks, target, place)


def prepare_kernel(hidden_ref, gain_ref, out_ref, gain_out_ref):
    gain_out_ref[...] = gain_ref[...]
    lane = lax.broadcasted_iota(jnp.int32, (16, 128), 1)
    for m in range(2):
        first, second = (hidden_ref[m, :, k : k + 128].astype(jnp.float32) for k in (0, 128))
        tail = jnp.pad(hidden_ref[m, :, 256:336].astype(jnp.float32), ((0, 0), (0, 48)))
        fold = jnp.concatenate([pltpu.roll(tail[16:24], 80, 1), pltpu.roll(tail[16:24], 40, 1)], axis=0)
        parts = [first[0:16], second[0:16], jnp.concatenate([first[16:24], second[16:24]], axis=0)]
        parts.append(jnp.where(lane < 80, tail[0:16], fold))
        for i, part in enumerate(parts):
            part = part.astype(jnp.bfloat16)
            for s in range(SOURCES):
                out_ref[2 * s + m, i * 16 : (i + 1) * 16, :] = part


def prepare(hidden, gain):
    return pl.pallas_call(
        prepare_kernel,
        out_shape=(
            jax.ShapeDtypeStruct((2 * SOURCES, 64, 128), jnp.bfloat16),
            jax.ShapeDtypeStruct((H,), jnp.float32),
        ),
        compiler_params=SMALL,
    )(*(pltpu.with_memory_space_constraint(a, pltpu.HBM) for a in (hidden, gain)))


def normalize_kernel(got_ref, gain_ref, out_ref, rows_ref):
    lane = lax.broadcasted_iota(jnp.int32, (24, 128), 1)
    scales = []
    for d in range(2):
        tiles = []
        for p in range(PARTS):
            block = [got_ref[d * PARTS + p, i * 16 : (i + 1) * 16, :].astype(jnp.float32) for i in range(4)]
            fold = block[3]
            unfolded = jnp.where(lane[0:8] < 40, pltpu.roll(fold[0:8], 48, 1), pltpu.roll(fold[8:16], 88, 1))
            whole = [(block[0], block[2][0:8]), (block[1], block[2][8:16]), (fold, unfolded)]
            tiles += [(p * PART + k * 128, jnp.concatenate(pair, axis=0)) for k, pair in enumerate(whole)]
        square = jnp.zeros((24, 128), jnp.float32)
        for t in range(H // 128):
            joined = None
            for begin, tile in tiles:
                width = 128 if begin % PART < 256 else 80
                at = begin - t * 128
                if at + width <= 0 or at >= 128:
                    continue
                moved = pltpu.roll(tile, at % 128, 1) if at % 128 else tile
                joined = moved if joined is None else jnp.where(lane >= at, moved, joined)
            rows_ref[d * 24 : (d + 1) * 24, t * 128 : (t + 1) * 128] = joined
            square = square + joined * joined
        scales.append(lax.rsqrt(jnp.sum(square, axis=1, keepdims=True) / H + epsilon))
    scale = jnp.concatenate(scales, axis=0)
    for t in range(H // 128):
        columns = slice(t * 128, (t + 1) * 128)
        out_ref[:, columns] = (rows_ref[:, columns] * scale * gain_ref[columns].reshape(1, 128)).astype(jnp.bfloat16)


def normalize(got, gain):
    return pl.pallas_call(
        normalize_kernel,
        out_shape=pltpu.HBM((OWN, H), jnp.bfloat16),
        scratch_shapes=[pltpu.VMEM((OWN, H), jnp.float32)],
        compiler_params=SMALL,
        cost_estimate=pl.CostEstimate(flops=2000000, bytes_accessed=1200000, transcendentals=0),
    )(got, gain)


def combine(peak, total, picked, axis):
    top = jnp.max(peak, axis=axis)
    total = jnp.sum(total * jnp.exp(peak - jnp.expand_dims(top, axis)), axis=axis)
    return top, total, jnp.sum(picked, axis=axis)


def per_device(hidden, norm_gain, embedding, targets):
    swap = [(0, 1), (1, 0)]
    tie = lax.optimization_barrier
    xh, xl, z, y, core = (lax.axis_index(a) for a in ("xh", "xl", "z", "y", "core"))

    x = xh * 2 + xl

    def first_row(at, c):
        return (((at % 4 * 8 + z) * 8 + y) * 2 + c) * VOCAB_LOCAL

    near = [first_row(x, c) + n * PIECE for c in (core, 1 - core) for n in range(2)]
    far = [first_row(x + 3 - 2 * n, c) + n * PIECE for c in (core, 1 - core) for n in range(2)]
    place = jnp.stack(near[:2] + far[:2] + near[2:] + far[2:])

    payload, gain = prepare(hidden, norm_gain)
    got = lax.all_to_all(payload, ("xh", "y", "core"), 0, 0, tiled=True)
    normed = normalize(got, gain)
    normed, late, asked = tie((normed, embedding, targets))
    rows = lax.all_gather(normed, "z", axis=0, tiled=True)

    from_left = lax.ppermute(late[:PIECE], ("xh", "xl"), [(i, (i + 1) % 4) for i in range(4)])
    from_right = lax.ppermute(late[PIECE:], ("xh", "xl"), [(i, (i - 1) % 4) for i in range(4)])
    beside = lax.ppermute(late, "core", swap)
    asked = jnp.broadcast_to(lax.dynamic_index_in_dim(asked, core, 0), (SOURCES, 24))
    target = lax.all_to_all(asked, ("z", "xh"), 0, 0, tiled=True).reshape(TOKENS, 1)
    from_left, from_right, target = tie((from_left, from_right, target))
    far = [from_left, from_right]
    far_beside = [lax.ppermute(part, "core", swap) for part in far]
    stats = local_losses(rows, (late, *far, beside, *far_beside), target, place)
    stats = stats[:3].reshape(3, SOURCES, 24).transpose(1, 0, 2)
    stats = lax.all_to_all(stats, ("z", "xh"), 0, 0, tiled=True)
    part = jnp.stack(combine(stats[:, 0], stats[:, 1], stats[:, 2], 0))
    every = lax.all_to_all(jnp.broadcast_to(part[None], (16, 3, 24)), ("y", "core"), 0, 0, tiled=True)
    every = every.reshape(PARTS // 2, 2, 3, 24)
    peak, total, picked = combine(every[:, :, 0], every[:, :, 1], every[:, :, 2], 0)
    return peak + jnp.log(total) - picked


def solution(mesh):
    fine = Mesh(mesh.devices.reshape(2, 2, 8, 8, 2), ("xh", "xl", "z", "y", "core"))
    dp, pipe = ("xh", "xl", "z"), ("y", "core")
    placed = (P(None, dp, pipe), P(), P(dp + pipe, None), P(None, dp))
    return jax.shard_map(per_device, mesh=fine, in_specs=placed, out_specs=P(None, dp), check_vma=False)
```

```python
import jax
import jax.numpy as jnp
import numpy as np
from jax import lax
from jax.experimental import pallas as pl
from jax.experimental.pallas import tpu as pltpu
from jax.sharding import Mesh
from jax.sharding import PartitionSpec as P

epsilon = 1e-06
H = 5376
PART = 336
PARTS = H // PART
SOURCES = 16
TOKENS = SOURCES * 24
OWN = 48
VOCAB_LOCAL = 256
WORDS = 4 * VOCAB_LOCAL
SMALL = pltpu.CompilerParams(vmem_limit_bytes=8 * 1024 * 1024)
PIECE = VOCAB_LOCAL // 2


def loss_kernel(*refs):
    rows_any, blocks = refs[0], refs[1:7]
    target_ref, place_ref, out_ref, xn, e, logits, x_sem, e_sem = refs[7:]
    x_copies = []
    for n in range(TOKENS // 96):
        rows = slice(n * 96, (n + 1) * 96)
        x_copies.append(pltpu.make_async_copy(rows_any.at[rows, :], xn.at[rows, :], x_sem.at[n]))
    e_copies, begin = [], 0
    for i, block in enumerate(blocks):
        words = slice(begin, begin + block.shape[0])
        begin += block.shape[0]
        e_copies.append(pltpu.make_async_copy(block, e.at[words, :], e_sem.at[i]))
    for copy in x_copies + e_copies:
        copy.start()
    for words, arrivals in ((slice(0, WORDS), x_copies + e_copies),):
        for copy in arrivals:
            copy.wait()
        logits[:, words] = lax.dot_general(
            xn[...], e[words, :], (((1,), (1,)), ((), ())), preferred_element_type=jnp.float32
        )

    lane = lax.broadcasted_iota(jnp.int32, (48, 128), 1)
    stats = []
    for step in range(TOKENS // 48):
        rows = pl.ds(step * 48, 48)
        parts = [logits[rows, i * 128 : (i + 1) * 128] for i in range(WORDS // 128)]
        peak = parts[0]
        for part in parts[1:]:
            peak = jnp.maximum(peak, part)
        peak = jnp.max(peak, axis=1, keepdims=True)
        target = target_ref[rows, :]
        total = jnp.zeros((48, 128), jnp.float32)
        picked = jnp.zeros((48, 128), jnp.float32)
        for i, part in enumerate(parts):
            total = total + jnp.exp(part - peak)
            picked = picked + jnp.where(target - place_ref[i] == lane, part, 0.0)
        total = jnp.sum(total, axis=1, keepdims=True)
        picked = jnp.sum(picked, axis=1, keepdims=True)
        stats.append(jnp.where(lane == 0, peak, jnp.where(lane == 1, total, picked)))
    stats = jnp.concatenate(stats, axis=0)
    for i in range(TOKENS // 128):
        out_ref[:, i * 128 : (i + 1) * 128] = stats[i * 128 : (i + 1) * 128, :].T[0:8, :]


def local_losses(rows, blocks, target, place):
    any_space = pl.BlockSpec(memory_space=pl.ANY)
    vmem = pl.BlockSpec(memory_space=pltpu.VMEM)
    rows = pltpu.with_memory_space_constraint(rows, pltpu.HBM)
    blocks = [pltpu.with_memory_space_constraint(a, pltpu.VMEM) for a in blocks]
    return pl.pallas_call(
        loss_kernel,
        out_shape=jax.ShapeDtypeStruct((8, TOKENS), jnp.float32),
        in_specs=[any_space] * 7 + [vmem, pl.BlockSpec(memory_space=pltpu.SMEM)],
        out_specs=vmem,
        scratch_shapes=[
            pltpu.VMEM((TOKENS, H), jnp.bfloat16),
            pltpu.VMEM((WORDS, H), jnp.bfloat16),
            pltpu.VMEM((TOKENS, WORDS), jnp.float32),
            pltpu.SemaphoreType.DMA((TOKENS // 96,)),
            pltpu.SemaphoreType.DMA((len(blocks),)),
        ],
        compiler_params=pltpu.CompilerParams(vmem_limit_bytes=24 * 1024 * 1024),
        cost_estimate=pl.CostEstimate(flops=2 * TOKENS * WORDS * H, bytes_accessed=16 * 1024 * 1024, transcendentals=TOKENS * WORDS),
    )(rows, *blocks, target, place)


def prepare_kernel(hidden_ref, gain_ref, out_ref, gain_out_ref):
    gain_out_ref[...] = gain_ref[...]
    lane = lax.broadcasted_iota(jnp.int32, (16, 128), 1)
    for m in range(2):
        first, second = (hidden_ref[m, :, k : k + 128].astype(jnp.float32) for k in (0, 128))
        tail = jnp.pad(hidden_ref[m, :, 256:336].astype(jnp.float32), ((0, 0), (0, 48)))
        fold = jnp.concatenate([pltpu.roll(tail[16:24], 80, 1), pltpu.roll(tail[16:24], 40, 1)], axis=0)
        parts = [first[0:16], second[0:16], jnp.concatenate([first[16:24], second[16:24]], axis=0)]
        parts.append(jnp.where(lane < 80, tail[0:16], fold))
        for i, part in enumerate(parts):
            part = part.astype(jnp.bfloat16)
            for s in range(SOURCES):
                out_ref[2 * s + m, i * 16 : (i + 1) * 16, :] = part


def prepare(hidden, gain):
    return pl.pallas_call(
        prepare_kernel,
        out_shape=(
            jax.ShapeDtypeStruct((2 * SOURCES, 64, 128), jnp.bfloat16),
            jax.ShapeDtypeStruct((H,), jnp.float32),
        ),
        compiler_params=SMALL,
    )(*(pltpu.with_memory_space_constraint(a, pltpu.HBM) for a in (hidden, gain)))


def normalize_kernel(got_ref, gain_ref, out_ref, rows_ref):
    lane = lax.broadcasted_iota(jnp.int32, (24, 128), 1)
    scales = []
    for d in range(2):
        tiles = []
        for p in range(PARTS):
            block = [got_ref[d * PARTS + p, i * 16 : (i + 1) * 16, :].astype(jnp.float32) for i in range(4)]
            fold = block[3]
            unfolded = jnp.where(lane[0:8] < 40, pltpu.roll(fold[0:8], 48, 1), pltpu.roll(fold[8:16], 88, 1))
            whole = [(block[0], block[2][0:8]), (block[1], block[2][8:16]), (fold, unfolded)]
            tiles += [(p * PART + k * 128, jnp.concatenate(pair, axis=0)) for k, pair in enumerate(whole)]
        square = jnp.zeros((24, 128), jnp.float32)
        for t in range(H // 128):
            joined = None
            for begin, tile in tiles:
                width = 128 if begin % PART < 256 else 80
                at = begin - t * 128
                if at + width <= 0 or at >= 128:
                    continue
                moved = pltpu.roll(tile, at % 128, 1) if at % 128 else tile
                joined = moved if joined is None else jnp.where(lane >= at, moved, joined)
            rows_ref[d * 24 : (d + 1) * 24, t * 128 : (t + 1) * 128] = joined
            square = square + joined * joined
        scales.append(lax.rsqrt(jnp.sum(square, axis=1, keepdims=True) / H + epsilon))
    scale = jnp.concatenate(scales, axis=0)
    for t in range(H // 128):
        columns = slice(t * 128, (t + 1) * 128)
        out_ref[:, columns] = (rows_ref[:, columns] * scale * gain_ref[columns].reshape(1, 128)).astype(jnp.bfloat16)


def normalize(got, gain):
    return pl.pallas_call(
        normalize_kernel,
        out_shape=pltpu.HBM((OWN, H), jnp.bfloat16),
        scratch_shapes=[pltpu.VMEM((OWN, H), jnp.float32)],
        compiler_params=SMALL,
        cost_estimate=pl.CostEstimate(flops=2000000, bytes_accessed=1200000, transcendentals=0),
    )(got, gain)


def combine(peak, total, picked, axis):
    top = jnp.max(peak, axis=axis)
    total = jnp.sum(total * jnp.exp(peak - jnp.expand_dims(top, axis)), axis=axis)
    return top, total, jnp.sum(picked, axis=axis)


def per_device(hidden, norm_gain, embedding, targets):
    swap = [(0, 1), (1, 0)]
    tie = lax.optimization_barrier
    xh, xl, z, y, core = (lax.axis_index(a) for a in ("xh", "xl", "z", "y", "core"))

    x = xh * 2 + xl

    def first_row(at, c):
        return (((at % 4 * 8 + z) * 8 + y) * 2 + c) * VOCAB_LOCAL

    near = [first_row(x, c) + n * PIECE for c in (core, 1 - core) for n in range(2)]
    far = [first_row(x + 3 - 2 * n, c) + n * PIECE for c in (core, 1 - core) for n in range(2)]
    place = jnp.stack(near[:2] + far[:2] + near[2:] + far[2:])

    payload, gain = prepare(hidden, norm_gain)
    got = lax.all_to_all(payload, ("xh", "y", "core"), 0, 0, tiled=True)
    normed = normalize(got, gain)
    normed, late, asked = tie((normed, embedding, targets))
    rows = lax.all_gather(normed, "z", axis=0, tiled=True)

    from_left = lax.ppermute(late[:PIECE], ("xh", "xl"), [(i, (i + 1) % 4) for i in range(4)])
    from_right = lax.ppermute(late[PIECE:], ("xh", "xl"), [(i, (i - 1) % 4) for i in range(4)])
    beside = lax.ppermute(late, "core", swap)
    asked = jnp.broadcast_to(lax.dynamic_index_in_dim(asked, core, 0), (SOURCES, 24))
    target = lax.all_to_all(asked, ("z", "xh"), 0, 0, tiled=True).reshape(TOKENS, 1)
    from_left, from_right, target = tie((from_left, from_right, target))
    far = [from_left, from_right]
    far_beside = [lax.ppermute(part, "core", swap) for part in far]
    stats = local_losses(rows, (late, *far, beside, *far_beside), target, place)
    stats = stats[:3].reshape(3, SOURCES, 24).transpose(1, 0, 2)
    stats = lax.all_to_all(stats, ("z", "xh"), 0, 0, tiled=True)
    part = jnp.stack(combine(stats[:, 0], stats[:, 1], stats[:, 2], 0))
    every = lax.all_to_all(jnp.broadcast_to(part[None], (16, 3, 24)), ("y", "core"), 0, 0, tiled=True)
    every = every.reshape(PARTS // 2, 2, 3, 24)
    peak, total, picked = combine(every[:, :, 0], every[:, :, 1], every[:, :, 2], 0)
    return peak + jnp.log(total) - picked


def solution(mesh):
    fine = Mesh(mesh.devices.reshape(2, 2, 8, 8, 2), ("xh", "xl", "z", "y", "core"))
    dp, pipe = ("xh", "xl", "z"), ("y", "core")
    placed = (P(None, dp, pipe), P(), P(dp + pipe, None), P(None, dp))
    return jax.shard_map(per_device, mesh=fine, in_specs=placed, out_specs=P(None, dp), check_vma=False)
```

```python
import jax
import jax.numpy as jnp
import numpy as np
from jax import lax
from jax.experimental import pallas as pl
from jax.experimental.pallas import tpu as pltpu
from jax.sharding import Mesh
from jax.sharding import PartitionSpec as P

epsilon = 1e-06
H = 5376
PART = 336
PARTS = H // PART
SOURCES = 16
TOKENS = SOURCES * 24
OWN = 48
VOCAB_LOCAL = 256
WORDS = 4 * VOCAB_LOCAL
SMALL = pltpu.CompilerParams(vmem_limit_bytes=8 * 1024 * 1024)
PIECE = VOCAB_LOCAL // 2


def loss_kernel(*refs):
    rows_any, blocks = refs[0], refs[1:7]
    target_ref, place_ref, out_ref, xn, e, logits, x_sem, e_sem = refs[7:]
    x_copies = []
    for n in range(TOKENS // 96):
        rows = slice(n * 96, (n + 1) * 96)
        x_copies.append(pltpu.make_async_copy(rows_any.at[rows, :], xn.at[rows, :], x_sem.at[n]))
    e_copies, begin = [], 0
    for i, block in enumerate(blocks):
        words = slice(begin, begin + block.shape[0])
        begin += block.shape[0]
        e_copies.append(pltpu.make_async_copy(block, e.at[words, :], e_sem.at[i]))
    for copy in x_copies + e_copies:
        copy.start()
    for words, arrivals in ((slice(0, WORDS // 2), x_copies + e_copies[:3]), (slice(WORDS // 2, WORDS), e_copies[3:])):
        for copy in arrivals:
            copy.wait()
        logits[:, words] = lax.dot_general(
            xn[...], e[words, :], (((1,), (1,)), ((), ())), preferred_element_type=jnp.float32
        )

    lane = lax.broadcasted_iota(jnp.int32, (48, 128), 1)
    stats = []
    for step in range(TOKENS // 48):
        rows = pl.ds(step * 48, 48)
        parts = [logits[rows, i * 128 : (i + 1) * 128] for i in range(WORDS // 128)]
        peak = parts[0]
        for part in parts[1:]:
            peak = jnp.maximum(peak, part)
        peak = jnp.max(peak, axis=1, keepdims=True)
        target = target_ref[rows, :]
        total = jnp.zeros((48, 128), jnp.float32)
        picked = jnp.zeros((48, 128), jnp.float32)
        for i, part in enumerate(parts):
            total = total + jnp.exp(part - peak)
            picked = picked + jnp.where(target - place_ref[i] == lane, part, 0.0)
        total = jnp.sum(total, axis=1, keepdims=True)
        picked = jnp.sum(picked, axis=1, keepdims=True)
        stats.append(jnp.where(lane == 0, peak, jnp.where(lane == 1, total, picked)))
    stats = jnp.concatenate(stats, axis=0)
    for i in range(TOKENS // 128):
        out_ref[:, i * 128 : (i + 1) * 128] = stats[i * 128 : (i + 1) * 128, :].T[0:8, :]


def local_losses(rows, blocks, target, place):
    any_space = pl.BlockSpec(memory_space=pl.ANY)
    vmem = pl.BlockSpec(memory_space=pltpu.VMEM)
    rows = pltpu.with_memory_space_constraint(rows, pltpu.HBM)
    blocks = [pltpu.with_memory_space_constraint(a, pltpu.VMEM) for a in blocks]
    return pl.pallas_call(
        loss_kernel,
        out_shape=jax.ShapeDtypeStruct((8, TOKENS), jnp.float32),
        in_specs=[any_space] * 7 + [vmem, pl.BlockSpec(memory_space=pltpu.SMEM)],
        out_specs=vmem,
        scratch_shapes=[
            pltpu.VMEM((TOKENS, H), jnp.bfloat16),
            pltpu.VMEM((WORDS, H), jnp.bfloat16),
            pltpu.VMEM((TOKENS, WORDS), jnp.float32),
            pltpu.SemaphoreType.DMA((TOKENS // 96,)),
            pltpu.SemaphoreType.DMA((len(blocks),)),
        ],
        compiler_params=pltpu.CompilerParams(vmem_limit_bytes=24 * 1024 * 1024),
        cost_estimate=pl.CostEstimate(flops=2 * TOKENS * WORDS * H, bytes_accessed=16 * 1024 * 1024, transcendentals=TOKENS * WORDS),
    )(rows, *blocks, target, place)


def prepare_kernel(hidden_ref, gain_ref, out_ref, gain_out_ref):
    gain_out_ref[...] = gain_ref[...]
    lane = lax.broadcasted_iota(jnp.int32, (16, 128), 1)
    for m in range(2):
        first, second = (hidden_ref[m, :, k : k + 128].astype(jnp.float32) for k in (0, 128))
        tail = jnp.pad(hidden_ref[m, :, 256:336].astype(jnp.float32), ((0, 0), (0, 48)))
        fold = jnp.concatenate([pltpu.roll(tail[16:24], 80, 1), pltpu.roll(tail[16:24], 40, 1)], axis=0)
        parts = [first[0:16], second[0:16], jnp.concatenate([first[16:24], second[16:24]], axis=0)]
        parts.append(jnp.where(lane < 80, tail[0:16], fold))
        for i, part in enumerate(parts):
            part = part.astype(jnp.bfloat16)
            for s in range(SOURCES):
                out_ref[2 * s + m, i * 16 : (i + 1) * 16, :] = part


def prepare(hidden, gain):
    return pl.pallas_call(
        prepare_kernel,
        out_shape=(
            jax.ShapeDtypeStruct((2 * SOURCES, 64, 128), jnp.bfloat16),
            jax.ShapeDtypeStruct((H,), jnp.float32),
        ),
        compiler_params=SMALL,
    )(*(pltpu.with_memory_space_constraint(a, pltpu.HBM) for a in (hidden, gain)))


def normalize_kernel(got_ref, gain_ref, out_any, rows_ref, out_ref, out_sem):
    lane = lax.broadcasted_iota(jnp.int32, (24, 128), 1)
    scales = []
    for d in range(2):
        tiles = []
        for p in range(PARTS):
            block = [got_ref[d * PARTS + p, i * 16 : (i + 1) * 16, :].astype(jnp.float32) for i in range(4)]
            fold = block[3]
            unfolded = jnp.where(lane[0:8] < 40, pltpu.roll(fold[0:8], 48, 1), pltpu.roll(fold[8:16], 88, 1))
            whole = [(block[0], block[2][0:8]), (block[1], block[2][8:16]), (fold, unfolded)]
            tiles += [(p * PART + k * 128, jnp.concatenate(pair, axis=0)) for k, pair in enumerate(whole)]
        square = jnp.zeros((24, 128), jnp.float32)
        for t in range(H // 128):
            joined = None
            for begin, tile in tiles:
                width = 128 if begin % PART < 256 else 80
                at = begin - t * 128
                if at + width <= 0 or at >= 128:
                    continue
                moved = pltpu.roll(tile, at % 128, 1) if at % 128 else tile
                joined = moved if joined is None else jnp.where(lane >= at, moved, joined)
            rows_ref[d * 24 : (d + 1) * 24, t * 128 : (t + 1) * 128] = joined
            square = square + joined * joined
        scales.append(lax.rsqrt(jnp.sum(square, axis=1, keepdims=True) / H + epsilon))
    scale = jnp.concatenate(scales, axis=0)
    copies = []
    for group in range(3):
        for t in range(group * 14, group * 14 + 14):
            columns = slice(t * 128, (t + 1) * 128)
            out_ref[:, columns] = (rows_ref[:, columns] * scale * gain_ref[columns].reshape(1, 128)).astype(jnp.bfloat16)
        done = slice(group * 1792, (group + 1) * 1792)
        copies.append(pltpu.make_async_copy(out_ref.at[:, done], out_any.at[:, done], out_sem.at[group]))
        copies[-1].start()
    for copy in copies:
        copy.wait()


def normalize(got, gain):
    return pl.pallas_call(
        normalize_kernel,
        out_shape=pltpu.HBM((OWN, H), jnp.bfloat16),
        out_specs=pl.BlockSpec(memory_space=pl.ANY),
        scratch_shapes=[
            pltpu.VMEM((OWN, H), jnp.float32),
            pltpu.VMEM((OWN, H), jnp.bfloat16),
            pltpu.SemaphoreType.DMA((3,)),
        ],
        compiler_params=SMALL,
        cost_estimate=pl.CostEstimate(flops=2000000, bytes_accessed=1200000, transcendentals=0),
    )(got, gain)


def combine(peak, total, picked, axis):
    top = jnp.max(peak, axis=axis)
    total = jnp.sum(total * jnp.exp(peak - jnp.expand_dims(top, axis)), axis=axis)
    return top, total, jnp.sum(picked, axis=axis)


def per_device(hidden, norm_gain, embedding, targets):
    swap = [(0, 1), (1, 0)]
    tie = lax.optimization_barrier
    xh, xl, z, y, core = (lax.axis_index(a) for a in ("xh", "xl", "z", "y", "core"))

    x = xh * 2 + xl

    def first_row(at, c):
        return (((at % 4 * 8 + z) * 8 + y) * 2 + c) * VOCAB_LOCAL

    near = [first_row(x, c) + n * PIECE for c in (core, 1 - core) for n in range(2)]
    far = [first_row(x + 3 - 2 * n, c) + n * PIECE for c in (core, 1 - core) for n in range(2)]
    place = jnp.stack(near[:2] + far[:2] + near[2:] + far[2:])

    payload, gain = prepare(hidden, norm_gain)
    got = lax.all_to_all(payload, ("xh", "y", "core"), 0, 0, tiled=True)
    normed = normalize(got, gain)
    normed, late, asked = tie((normed, embedding, targets))
    rows = lax.all_gather(normed, "z", axis=0, tiled=True)

    from_left = lax.ppermute(late[:PIECE], ("xh", "xl"), [(i, (i + 1) % 4) for i in range(4)])
    from_right = lax.ppermute(late[PIECE:], ("xh", "xl"), [(i, (i - 1) % 4) for i in range(4)])
    beside = lax.ppermute(late, "core", swap)
    asked = jnp.broadcast_to(lax.dynamic_index_in_dim(asked, core, 0), (SOURCES, 24))
    target = lax.all_to_all(asked, ("z", "xh"), 0, 0, tiled=True).reshape(TOKENS, 1)
    from_left, from_right, target = tie((from_left, from_right, target))
    far = [from_left, from_right]
    far_beside = [lax.ppermute(part, "core", swap) for part in far]
    stats = local_losses(rows, (late, *far, beside, *far_beside), target, place)
    stats = stats[:3].reshape(3, SOURCES, 24).transpose(1, 0, 2)
    stats = lax.all_to_all(stats, ("z", "xh"), 0, 0, tiled=True)
    part = jnp.stack(combine(stats[:, 0], stats[:, 1], stats[:, 2], 0))
    every = lax.all_to_all(jnp.broadcast_to(part[None], (16, 3, 24)), ("y", "core"), 0, 0, tiled=True)
    every = every.reshape(PARTS // 2, 2, 3, 24)
    peak, total, picked = combine(every[:, :, 0], every[:, :, 1], every[:, :, 2], 0)
    return peak + jnp.log(total) - picked


def solution(mesh):
    fine = Mesh(mesh.devices.reshape(2, 2, 8, 8, 2), ("xh", "xl", "z", "y", "core"))
    dp, pipe = ("xh", "xl", "z"), ("y", "core")
    placed = (P(None, dp, pipe), P(), P(dp + pipe, None), P(None, dp))
    return jax.shard_map(per_device, mesh=fine, in_specs=placed, out_specs=P(None, dp), check_vma=False)
```
